256 devices in a mesh: worker: 8 (over x, z_lo), fsdp: 32 (over y, z_hi, core).
Axes of the slice: x: 4, y: 4, z: 8 (z_hi: 4, z_lo: 2; z = z_hi * 2 + z_lo), core: 2. Of those that a mesh axis runs over, the one named last changes fastest.
Arguments:
- tokens: bfloat16 [8, 8192, 7168], P('worker', 'fsdp'), may hold values from -6 to 6
- norm_gain: float32 [8, 7168], P('worker'), may hold values from 0.5 to 1.5
- value_weight: bfloat16 [8, 7168, 512], P('worker', 'fsdp'), may hold values from -0.0625 to 0.0625
- value_cotangent: bfloat16 [8, 8192, 512], P('worker', 'fsdp'), may hold values from -3 to 3
- local_fragments: float32 [8, 16, 524288], P('worker', None, 'fsdp'), may hold values from -6 to 6
- global_fragments: float32 [16, 524288], P(None, 'fsdp'), may hold values from -6 to 6
- outer_velocity: float32 [16, 524288], P(None, 'fsdp'), may hold values from -6 to 6
- fragment_index: int32 [1], replicated, may hold values from 0 to 15
Outputs:
- token_grad: bfloat16 [8, 8192, 7168], P('worker', 'fsdp')
- weight_grad: float32 [8, 7168, 512], P('worker', 'fsdp')
- gain_grad: float32 [8, 7168], P('worker', 'fsdp')
- outer_param: float32 [524288], P('fsdp')
- outer_momentum: float32 [524288], P('fsdp')
The draws below stay inside these ranges and needn't reach their ends.
All inputs are finite; a program needn't handle non-finite values.
Results may differ from the reference program's by a relative error of at most 0.0031.
Values may be sent and summed in bfloat16 or wider, within the bound.
A program may use at most 128 MiB of HBM per device.

```python
import jax
import jax.numpy as jnp
from jax import lax

D = 7168
KV = 512
NFRAG = 16
GROUPS = 8
GROUP_TOK = 8192
FRAG = 524288


def level_of(rng, extent, split, least, high):
    def one(axis_at, shards_of):
        draws = jax.random.uniform(jax.random.fold_in(jax.random.fold_in(rng, 6), axis_at), (shards_of,), jnp.float32, least / len(split), high / len(split))
        return jnp.repeat(jnp.exp(draws), extent[axis_at] // shards_of).reshape((-1,) + (1,) * (len(extent) - axis_at - 1))

    gain = one(*split[0])
    for cut in split[1:]:
        gain = gain * one(*cut)
    return gain


def bell_draw(key, extent, deviation, most, pieces=(), kind=jnp.bfloat16):
    values = deviation * jax.random.normal(key, extent, jnp.float32)
    if pieces:
        values = values * level_of(key, extent, pieces, -0.22, 0.18)
    return jnp.clip(values, -most, most).astype(kind)


def setup_inputs(seed: int = 0) -> dict:
    splits = jax.random.split(jax.random.key(seed), 9)
    return {
        "tokens": bell_draw(splits[0], (GROUPS, GROUP_TOK, D), 1.0, 6.0, ((0, 8), (1, 32))),
        "norm_gain": jnp.clip(1.0 + 0.1 * jax.random.normal(splits[1], (GROUPS, D), jnp.float32), 0.5, 1.5),
        "value_weight": bell_draw(splits[2], (GROUPS, D, KV), D ** -0.5, 0.0625, ((0, 8), (1, 32))),
        "value_cotangent": bell_draw(splits[3], (GROUPS, GROUP_TOK, KV), 0.5, 3.0, ((0, 8), (1, 32))),
        "local_fragments": bell_draw(splits[4], (GROUPS, NFRAG, FRAG), 1.0, 6.0, ((0, 8), (2, 32)), jnp.float32),
        "global_fragments": bell_draw(splits[5], (NFRAG, FRAG), 1.0, 6.0, ((1, 32),), jnp.float32),
        "outer_velocity": bell_draw(splits[6], (NFRAG, FRAG), 1.0, 6.0, ((1, 32),), jnp.float32),
        "fragment_index": jax.random.randint(splits[7], (1,), 0, NFRAG).astype(jnp.int32),
    }


EPSILON = 1e-05
MOMENTUM = 0.9
OUTER_RATE = 0.7

def reference(tokens, norm_gain, value_weight, value_cotangent, local_fragments, global_fragments, outer_velocity, fragment_index):
    token_list = []
    weight_list = []
    gain_list = []
    for replica in range(GROUPS):
        widened = tokens[replica].astype(jnp.float32)
        inverse = lax.rsqrt(lax.optimization_barrier(jnp.mean(widened * widened, axis=1, keepdims=True)) + EPSILON)
        normed = (widened * inverse * norm_gain[replica][None, :]).astype(jnp.bfloat16)
        upstream = value_cotangent[replica]
        d_normed = jnp.dot(upstream, value_weight[replica].T, preferred_element_type=jnp.float32)
        gain_list.append(lax.optimization_barrier(jnp.sum(d_normed * widened * inverse, axis=0)))
        weight_list.append(jnp.dot(normed.T, upstream, preferred_element_type=jnp.float32))
        scaled = d_normed * norm_gain[replica][None, :]
        projected = lax.optimization_barrier(jnp.mean(scaled * widened, axis=1, keepdims=True))
        token_list.append((inverse * (scaled - widened * inverse * inverse * projected)).astype(jnp.bfloat16))
    chosen = fragment_index[0].astype(jnp.int32)
    anchor = lax.dynamic_index_in_dim(global_fragments, chosen, 0, keepdims=False)
    replica_part = lax.dynamic_index_in_dim(local_fragments, chosen, 1, keepdims=False)
    velocity = lax.dynamic_index_in_dim(outer_velocity, chosen, 0, keepdims=False)
    pseudo_grad = lax.optimization_barrier(jnp.sum(anchor[None, :] - replica_part, axis=0)) / GROUPS
    outer_momentum = MOMENTUM * velocity + pseudo_grad
    outer_param = anchor - OUTER_RATE * (pseudo_grad + MOMENTUM * outer_momentum)
    return (jnp.stack(token_list), jnp.stack(weight_list), jnp.stack(gain_list), outer_param, outer_momentum)
```

```python
import functools

import jax
import jax.numpy as jnp
from jax import lax
from jax.experimental import pallas as pl
from jax.experimental.pallas import tpu as pltpu
from jax.sharding import PartitionSpec as P

EPSILON = 1e-05
MOMENTUM = 0.9
OUTER_RATE = 0.7
MESH = pl.DeviceIdType.MESH
RING = 4
NT = (((1,), (1,)), ((), ()))
SEMS = 120
GATHER_PARTS = ((0, 224, "z"),)
SCATTER_PARTS = ((0, 128, "y"), (128, 224, "z"))


def kernel(
    tokens,
    gain,
    weight,
    cotangent,
    difference,
    anchor,
    velocity,
    token_out,
    weight_out,
    gain_out,
    param_out,
    momentum_out,
    tok,
    turned,
    turned_other,
    cot,
    full,
    part,
    scaled,
    inverse,
    projected,
    x_in,
    z_out,
    z_in,
    *rest,
):
    buffers, (send_sem, recv_sem, local_sem) = rest[:-3], rest[-3:]
    rows, features = tok.shape
    block = weight.shape[0]
    values = weight.shape[1]

    worker = lax.axis_index("worker")
    place = lax.axis_index("fsdp")
    core = lax.rem(place, 2)
    z = lax.rem(place // 2, RING)
    y = place // (2 * RING)
    x, low = worker // 2, lax.rem(worker, 2)

    chip = {
        (dy, dz): lax.rem(y + dy, RING) * RING + lax.rem(z + dz, RING)
        for dy in range(RING)
        for dz in range(RING)
    }

    def device(dy, dz):
        return {"fsdp": 2 * chip[dy, dz] + core}

    partner = {"fsdp": place + 1 - 2 * core}
    beside_x = [{"worker": lax.rem(x + d, RING) * 2 + low} for d in (1, 2, 3)]
    beside_low = {"worker": x * 2 + 1 - low}

    numbers = {}

    def copy(key, src, dst, target):
        index = numbers.setdefault(key, len(numbers))
        return pltpu.make_async_remote_copy(
            src_ref=src,
            dst_ref=dst,
            send_sem=send_sem.at[index],
            recv_sem=recv_sem.at[index],
            device_id=target,
            device_id_type=MESH,
        )

    sent = []

    def send(key, src, dst, target):
        c = copy(key, src, dst, target)
        c.start()
        sent.append(c)

    def arrive(key, dst, target):
        copy(key, dst, dst, target).wait_recv()

    token_copies = []
    half_rows = rows // 2
    for i in range(2):
        span = pl.ds(i * half_rows, half_rows)
        token_copies.append(
            pltpu.make_async_copy(tokens.at[span], tok.at[span], local_sem.at[i])
        )
    cot_copy = pltpu.make_async_copy(cotangent, cot.at[0], local_sem.at[2])
    own = pl.ds(pl.multiple_of(place * block, 16), block)
    own_copy = pltpu.make_async_copy(weight, full.at[own], local_sem.at[3])
    for c in token_copies:
        c.start()
    cot_copy.start()
    own_copy.start()

    greeted = [partner, *beside_x, beside_low]
    greeted += [device(1, 0), device(3, 0), device(0, 1), device(0, 3)]
    barrier = pltpu.get_barrier_semaphore()
    for target in greeted:
        pl.semaphore_signal(barrier, inc=1, device_id=target, device_id_type=MESH)
    pl.semaphore_wait(barrier, len(greeted))

    events = []

    def at(time, fn, *args):
        events.append((time, len(events), functools.partial(fn, *args)))

    def slot(dy, dz, which, lo, hi):
        start = (2 * chip[dy, dz] + which) * block + lo
        return full.at[pl.ds(pl.multiple_of(start, 16), hi - lo)]

    def gather(number, lo, hi, first, times):
        mid = (lo + hi) // 2
        halves = {1: (lo, mid), 3: (mid, hi)}

        def at_offset(a, b):
            return (b, a) if first == "z" else (a, b)

        def to_first(s):
            return device(*at_offset(s, 0))

        def to_second(s):
            return device(*at_offset(0, s))

        def held(a, b, which=core, span=(lo, hi)):
            return slot(*at_offset(a, b), which, *span)

        def exchange(a, b, src=None):
            here = held(a, b)
            send((number, "x", a, b), here if src is None else src, here, partner)

        def spread(a, src=None):
            here = held(a, 0)
            for s in (1, 3):
                send((number, "b", a, s), here if src is None else src, here, to_second(s))

        def begin():
            src = weight.at[pl.ds(lo, hi - lo)]
            for s in (1, 3):
                send((number, "a", s), src, held(0, 0), to_first(s))
            spread(0, src)
            exchange(0, 0, src)

        def first_near():
            for s in (1, 3):
                arrive((number, "a", s), held(4 - s, 0), to_first(s))
                piece = held(4 - s, 0, core, halves[s])
                send((number, "af", s), piece, piece, to_first(s))
            for s in (1, 3):
                spread(4 - s)
            for s in (1, 3):
                exchange(4 - s, 0)

        def first_far():
            for s in (1, 3):
                arrive((number, "af", s), held(2, 0, core, halves[s]), to_first(s))
            spread(2)
            exchange(2, 0)

        def second_near(a):
            for s in (1, 3):
                arrive((number, "b", a, s), held(a, 4 - s), to_second(s))
                piece = held(a, 4 - s, core, halves[s])
                send((number, "bf", a, s), piece, piece, to_second(s))
            for s in (1, 3):
                exchange(a, 4 - s)

        def second_far(a):
            for s in (1, 3):
                arrive((number, "bf", a, s), held(a, 2, core, halves[s]), to_second(s))
            exchange(a, 2)

        def settled(dy):
            for dz in range(RING):
                a, b = (dz, dy) if first == "z" else (dy, dz)
                arrive((number, "x", a, b), held(a, b, 1 - core), partner)

        at(times["begin"], begin)
        at(times["first_near"], first_near)
        at(times["first_far"], first_far)
        for a in (0, 3, 1, 2):
            at(times["near"][a], second_near, a)
            at(times["far"][a], second_far, a)
        return settled

    span = features // RING

    def project(dy):
        start = pl.multiple_of(lax.rem(y + dy, RING) * span, 128)

        @pl.loop(0, span // 256)
        def _(i):
            here = pl.ds(pl.multiple_of(start + i * 256, 128), 256)
            d = lax.dot_general(
                cot[0], full[here, :], NT, preferred_element_type=jnp.float32
            )
            s = d * gain[:, here]
            scaled[:, here] = s
            both = s * tok[:, here].astype(jnp.float32)
            projected[...] += both[:, :128] + both[:, 128:]

    def finish_tokens():
        step = 32

        @pl.loop(0, rows // step)
        def _(i):
            here = pl.ds(pl.multiple_of(i * step, step), step)
            inv = inverse[here, :]
            mean = jnp.sum(projected[here, :], axis=1, keepdims=True) / features
            back = inv * inv * mean

            @pl.loop(0, features // 1024)
            def _(j):
                cols = pl.ds(pl.multiple_of(j * 1024, 128), 1024)
                wide = tok[here, cols].astype(jnp.float32)
                tok[here, cols] = (inv * (scaled[here, cols] - wide * back)).astype(
                    jnp.bfloat16
                )

            pltpu.make_async_copy(tok.at[here], token_out.at[here], local_sem.at[4]).start()

        pltpu.make_async_copy(tok, token_out, local_sem.at[4]).wait()

    def normalize():
        for i in range(2):
            token_copies[i].wait()
            here = pl.ds(i * half_rows, half_rows)

            def square(j, total):
                wide = tok[here, pl.ds(pl.multiple_of(j * 256, 128), 256)].astype(
                    jnp.float32
                )
                wide = wide * wide
                return total + wide[:, :128] + wide[:, 128:]

            total = lax.fori_loop(
                0, features // 256, square, jnp.zeros((half_rows, 128), jnp.float32)
            )
            inv = lax.rsqrt(jnp.sum(total, axis=1, keepdims=True) / features + EPSILON)
            inverse[here, :] = inv

            @pl.loop(0, features // (4 * block))
            def _(j):
                cols = pl.ds(pl.multiple_of(j * 4 * block, 128), 4 * block)
                normed = (
                    tok[here, cols].astype(jnp.float32) * inv * gain[:, cols]
                ).astype(jnp.bfloat16)
                flipped = normed.T
                for b in range(4):
                    turned[2 * j + b // 2, b % 2, :, here] = flipped[
                        b * block : (b + 1) * block
                    ]

        for q in range(RING):
            here = pl.ds(q * RING, RING)
            send(("t", q), turned.at[here, 1 - core], turned_other.at[here], partner)

    def own_products():
        cot_copy.wait()

        @pl.loop(0, RING * RING)
        def _(k):
            part[k] = jnp.dot(
                turned[k, core], cot[0], preferred_element_type=jnp.float32
            )

    def other_products():
        arrive("cot", cot.at[1], partner)
        for q in range(RING):
            arrive(("t", q), turned_other.at[pl.ds(q * RING, RING)], partner)

        @pl.loop(0, RING * RING)
        def _(k):
            part[k] += jnp.dot(
                turned_other[k], cot[1], preferred_element_type=jnp.float32
            )

    def scatter(number, lo, hi, first, refs, times):
        far_out, far_in, near_out, near_in, far2_out, far2_in, near2_out, near2_in, total = (
            refs
        )
        size = hi - lo
        halves = {1: pl.ds(0, size // 2), 3: pl.ds(size // 2, size // 2)}
        other = {1: halves[3], 3: halves[1]}
        index = {1: 0, 3: 1}
        start = {1: lo, 3: lo + size // 2}

        def at_offset(a, b):
            return (b, a) if first == "z" else (a, b)

        def to_first(s):
            return device(*at_offset(s, 0))

        def to_second(s):
            return device(*at_offset(0, s))

        def mine(a, b, s=None):
            span = pl.ds(lo, size) if s is None else pl.ds(start[s], size // 2)
            return part[chip[at_offset(a, b)], span, :]

        def far(b):
            for s in (1, 3):
                far_out[b, halves[s], :] = mine(2, b, s).astype(jnp.bfloat16)
                send(
                    (number, "f", b, s),
                    far_out.at[b, halves[s]],
                    far_in.at[b, halves[s]],
                    to_first(s),
                )

        def near(b):
            for s in (1, 3):
                i = index[s]
                near_out[i, b, other[s], :] = mine(s, b, 4 - s).astype(jnp.bfloat16)
                arrive((number, "f", b, s), far_in.at[b, halves[s]], to_first(s))
                near_out[i, b, halves[s], :] = (
                    mine(s, b, s) + far_in[b, halves[s], :].astype(jnp.float32)
                ).astype(jnp.bfloat16)
                send((number, "n", b, s), near_out.at[i, b], near_in.at[i, b], to_first(s))

        def gathered(b):
            for s in (1, 3):
                arrive((number, "n", b, s), near_in.at[index[s], b], to_first(s))
            total[b] = (
                mine(0, b)
                + near_in[0, b].astype(jnp.float32)
                + near_in[1, b].astype(jnp.float32)
            )

        def far2():
            for s in (1, 3):
                far2_out[halves[s], :] = total[2, halves[s], :].astype(jnp.bfloat16)
                send(
                    (number, "f2", s),
                    far2_out.at[halves[s]],
                    far2_in.at[halves[s]],
                    to_second(s),
                )

        def near2(s):
            i = index[s]
            near2_out[i, other[s], :] = total[s, other[s], :].astype(jnp.bfloat16)
            arrive((number, "f2", s), far2_in.at[halves[s]], to_second(s))
            near2_out[i, halves[s], :] = (
                total[s, halves[s], :] + far2_in[halves[s], :].astype(jnp.float32)
            ).astype(jnp.bfloat16)
            send((number, "n2", s), near2_out.at[i], near2_in.at[i], to_second(s))

        def final():
            for s in (1, 3):
                arrive((number, "n2", s), near2_in.at[index[s]], to_second(s))
            weight_out[pl.ds(lo, size), :] = (
                total[0]
                + near2_in[0].astype(jnp.float32)
                + near2_in[1].astype(jnp.float32)
            )

        order = (2, 1, 3, 0)
        for j, b in enumerate(order):
            at(times["far"][j], far, b)
            at(times["near"][j], near, b)
            at(times["sum"][j], gathered, b)
        at(times["sum"][0] + 0.01, far2)
        at(times["sum"][1] + 0.01, near2, 1)
        at(times["sum"][2] + 0.01, near2, 3)
        at(times["final"], final)

    def gain_gradient():
        product = weight_out[...] * full[own, :].astype(jnp.float32)
        ones = jnp.ones((8, values), jnp.float32)
        sums = lax.dot_general(
            ones,
            product,
            NT,
            preferred_element_type=jnp.float32,
            precision=lax.Precision.HIGHEST,
        )[0:1]
        group = gain[:, pl.ds(pl.multiple_of((place // 4) * 4 * block, 128), 4 * block)]
        which = lax.rem(place, 4)
        scale = group[:, :block]
        for i in range(1, 4):
            scale = jnp.where(which == i, group[:, i * block : (i + 1) * block], scale)
        gain_out[...] = sums / scale

    def outer_begin():
        x_in[x] = difference[...]
        for i, target in enumerate(beside_x):
            send(("ox", i), difference, x_in.at[x], target)

    def outer_middle():
        for i, target in enumerate(beside_x):
            arrive(("ox", i), x_in.at[lax.rem(x + RING - 1 - i, RING)], target)
        z_out[...] = x_in[0] + x_in[1] + x_in[2] + x_in[3]
        send("oz", z_out, z_in, beside_low)

    def outer_end():
        arrive("oz", z_in, beside_low)
        pseudo = (z_out[...] + z_in[...]) / 8
        momentum = MOMENTUM * velocity[...] + pseudo
        momentum_out[...] = momentum
        param_out[...] = anchor[...] - OUTER_RATE * (pseudo + MOMENTUM * momentum)

    def send_cotangent():
        send("cot", cotangent, cot.at[1], partner)

    def clear():
        projected[...] = jnp.zeros_like(projected)

    settled = []
    settled.append(
        gather(
            "g0",
            *GATHER_PARTS[0],
            dict(
                begin=0,
                first_near=9.5,
                first_far=14,
                near={0: 6, 3: 16.5, 1: 16.6, 2: 27},
                far={0: 9, 3: 23.5, 1: 23.6, 2: 32},
            ),
        )
    )
    at(0.5, send_cotangent)
    at(0.6, outer_begin)
    at(1, clear)
    at(2, normalize)
    at(7, own_products)
    at(9.4, other_products)
    scatter(
        "s0",
        *SCATTER_PARTS[0],
        buffers[:9],
        dict(far=(10, 10.1, 15, 22), near=(13, 17, 25, 31), sum=(21, 28, 34, 38), final=46),
    )
    scatter(
        "s1",
        *SCATTER_PARTS[1],
        buffers[9:],
        dict(far=(10.2, 10.3, 17.1, 24), near=(14.1, 20, 26, 31.2), sum=(22, 29, 35, 39), final=45),
    )
    at(20, outer_middle)
    at(30, outer_end)

    def settle_and_project(dy):
        for fn in settled:
            fn(dy)
        project(dy)

    at(19, lambda: own_copy.wait())
    at(19.1, settle_and_project, 0)
    at(40, settle_and_project, 3)
    at(40.1, settle_and_project, 1)
    at(40.2, settle_and_project, 2)
    at(40.3, finish_tokens)

    at(47, gain_gradient)
    for _, _, fn in sorted(events, key=lambda e: e[:2]):
        fn()
    for c in sent:
        c.wait_send()


def local(
    tokens,
    norm_gain,
    value_weight,
    value_cotangent,
    local_fragments,
    global_fragments,
    outer_velocity,
    fragment_index,
):
    chosen = fragment_index[0]
    anchor = lax.dynamic_index_in_dim(global_fragments, chosen, 0, keepdims=False)
    replica_part = lax.dynamic_index_in_dim(local_fragments[0], chosen, 0, keepdims=False)
    velocity = lax.dynamic_index_in_dim(outer_velocity, chosen, 0, keepdims=False)
    square = (-1, 128)
    anchor, velocity = anchor.reshape(square), velocity.reshape(square)
    difference = anchor - replica_part.reshape(square)
    lines = anchor.shape[0]

    _, rows, features = tokens.shape
    _, block, values = value_weight.shape
    blocks = RING * RING
    vmem = pltpu.VMEM
    bf16, f32 = jnp.bfloat16, jnp.float32
    scratch = [
        vmem((rows, features), bf16),
        vmem((blocks, 2, block, rows), bf16),
        vmem((blocks, block, rows), bf16),
        vmem((2, rows, values), bf16),
        vmem((features, values), bf16),
        vmem((blocks, block, values), f32),
        vmem((rows, features), f32),
        vmem((rows, 1), f32),
        vmem((rows, 128), f32),
        vmem((RING, lines, 128), f32),
        vmem((lines, 128), f32),
        vmem((lines, 128), f32),
    ]
    for lo, hi, _ in SCATTER_PARTS:
        size = hi - lo
        scratch += [
            vmem((RING, size, values), bf16),
            vmem((RING, size, values), bf16),
            vmem((2, RING, size, values), bf16),
            vmem((2, RING, size, values), bf16),
            vmem((size, values), bf16),
            vmem((size, values), bf16),
            vmem((2, size, values), bf16),
            vmem((2, size, values), bf16),
            vmem((RING, size, values), f32),
        ]
    scratch += [
        pltpu.SemaphoreType.DMA((SEMS,)),
        pltpu.SemaphoreType.DMA((SEMS,)),
        pltpu.SemaphoreType.DMA((5,)),
    ]
    in_vmem = pl.BlockSpec(memory_space=pltpu.VMEM)
    in_hbm = pl.BlockSpec(memory_space=pl.ANY)
    token_grad, weight_grad, gain_grad, param, momentum = pl.pallas_call(
        kernel,
        out_shape=(
            jax.ShapeDtypeStruct((rows, features), bf16),
            jax.ShapeDtypeStruct((block, values), f32),
            jax.ShapeDtypeStruct((1, block), f32),
            jax.ShapeDtypeStruct((lines, 128), f32),
            jax.ShapeDtypeStruct((lines, 128), f32),
        ),
        in_specs=[in_hbm, in_vmem, in_hbm, in_hbm, in_vmem, in_vmem, in_vmem],
        out_specs=(in_hbm, in_vmem, in_vmem, in_vmem, in_vmem),
        scratch_shapes=scratch,
        compiler_params=pltpu.CompilerParams(
            collective_id=0, has_side_effects=True, vmem_limit_bytes=58 * 2**20
        ),
        cost_estimate=pl.CostEstimate(
            flops=4 * rows * features * values, bytes_accessed=2**24, transcendentals=0
        ),
    )(
        tokens[0],
        norm_gain,
        value_weight[0],
        value_cotangent[0],
        difference,
        anchor,
        velocity,
    )
    return (
        token_grad[None],
        weight_grad[None],
        gain_grad,
        param.reshape(-1),
        momentum.reshape(-1),
    )


def solution(mesh):
    placed = (
        P("worker", "fsdp", None),
        P("worker", None),
        P("worker", "fsdp", None),
        P("worker", "fsdp", None),
        P("worker", None, "fsdp"),
        P(None, "fsdp"),
        P(None, "fsdp"),
        P(),
    )
    return jax.shard_map(
        local,
        mesh=mesh,
        in_specs=placed,
        out_specs=(
            P("worker", "fsdp", None),
            P("worker", "fsdp", None),
            P("worker", "fsdp"),
            P("fsdp"),
            P("fsdp"),
        ),
        check_vma=False,
    )
```

```python
import functools
import types

import jax
import jax.numpy as jnp
from jax import lax
from jax.experimental import pallas as pl
from jax.experimental.pallas import tpu as pltpu
from jax.sharding import PartitionSpec as P

EPSILON = 1e-05
MOMENTUM = 0.9
OUTER_RATE = 0.7
MESH = pl.DeviceIdType.MESH
RING = 4
NT = (((1,), (1,)), ((), ()))
GATHER_PARTS = ((0, 64, "z"), (64, 128, "z"), (128, 224, "z"))
SCATTER_PARTS = ((0, 64, "y"), (64, 128, "y"), (128, 224, "z"))
WIDTH = 512
ORDER = (
    0, 32, 16, 48, 49, 4, 50, 52, 54, 5, 1, 2, 20, 21, 51, 106, 86, 66, 56, 6, 58, 33, 8, 34,
    126, 11, 10, 22, 18, 17, 129, 36, 53, 3, 67, 110, 55, 114, 68, 127, 57, 59, 118, 90, 42, 39,
    35, 87, 12, 107, 19, 26, 27, 70, 108, 94, 24, 74, 43, 37, 13, 14, 88, 40, 23, 69, 82, 7, 60,
    62, 64, 128, 46, 61, 112, 63, 115, 30, 45, 65, 72, 111, 132, 116, 76, 29, 28, 44, 71, 109,
    122, 38, 95, 75, 96, 15, 133, 120, 25, 89, 102, 9, 41, 92, 119, 47, 91, 134, 31, 73, 83,
    135, 98, 136, 113, 123, 78, 137, 77, 84, 97, 117, 124, 93, 103, 99, 100, 104, 130, 80, 121,
    79, 131, 138, 140, 101, 125, 81, 85, 105, 139,
)
OPPOSITE = {1: 3, 3: 1, 2: 2}
CHUNKS = ((2, 1), (1, 1), (3, 1), (2, 0), (0, 1), (1, 0), (3, 0), (0, 0))


class Event:
    def __init__(self, name, body, cost, rank, needs=(), after=(), sends=()):
        self.name, self.body, self.cost, self.rank = name, body, cost, rank
        self.needs, self.after, self.sends = list(needs), list(after), list(sends)


def build(env, rows, features, block):
    events = []

    def add(name, *args, **kw):
        events.append(Event(name, *args, **kw))

    def nothing():
        pass

    chunk_of = {c: i for i, c in enumerate(CHUNKS)}

    def product(dy, dz):
        sides = {0: (0,), 2: (1,), 1: (0, 1), 3: (0, 1)}[dz]
        return [("product", chunk_of[dy, s]) for s in sides]

    def gather(number, lo, hi, first):
        mid = (lo + hi) // 2
        halves = {1: (lo, mid), 3: (mid, hi)}
        second = "y" if first == "z" else "z"
        full_size, half_size = (hi - lo) * WIDTH * 2, (hi - lo) * WIDTH

        def offset(a, b):
            return (b, a) if first == "z" else (a, b)

        def target(axis, s):
            return env.device(0, s) if axis == "z" else env.device(s, 0)

        def held(a, b, span=(lo, hi), other=False):
            which = 1 - env.core if other else env.core
            return env.slot(*offset(a, b), which, *span)

        def whole(key, axis, s, a, b, own=False):
            def refs():
                here = held(a, b)
                src = env.weight.at[pl.ds(lo, hi - lo)] if own else here
                return src, here, target(axis, s)

            return (number, *key), axis + str(s), full_size, refs

        def half(key, axis, s, a, b):
            def refs():
                here = held(a, b, halves[s])
                return here, here, target(axis, s)

            return (number, *key), axis + str(s), half_size, refs

        def exchange(a, b, own=False):
            def refs():
                here = held(a, b)
                src = env.weight.at[pl.ds(lo, hi - lo)] if own else here
                return src, here, env.partner

            return (number, "x", a, b), "c", full_size, refs

        def need(key, axis, s, a, b, part=False):
            def refs():
                return held(a, b, halves[s] if part else (lo, hi)), target(axis, s)

            return (number, *key), refs

        def spread(a, own=False):
            return [whole(("b", a, s), second, s, a, 0, own) for s in (1, 3)]

        add(
            (number, "begin"),
            nothing,
            0.1,
            0,
            sends=[whole(("a", s), first, s, 0, 0, True) for s in (1, 3)]
            + spread(0, True)
            + [exchange(0, 0, True)],
        )
        for s in (1, 3):
            a = OPPOSITE[s]
            add(
                (number, "first", s),
                nothing,
                0.1,
                1,
                needs=[need(("a", s), first, s, a, 0)],
                sends=[half(("af", s), first, s, a, 0), *spread(a), exchange(a, 0)],
            )
        add(
            (number, "first", 2),
            nothing,
            0.1,
            1,
            needs=[need(("af", s), first, s, 2, 0, True) for s in (1, 3)],
            sends=[*spread(2), exchange(2, 0)],
        )
        for a in (0, 3, 1, 2):
            for s in (1, 3):
                b = OPPOSITE[s]
                add(
                    (number, "second", a, s),
                    nothing,
                    0.1,
                    1,
                    needs=[need(("b", a, s), second, s, a, b)],
                    sends=[half(("bf", a, s), second, s, a, b), exchange(a, b)],
                )
            add(
                (number, "second", a, 2),
                nothing,
                0.1,
                1,
                needs=[need(("bf", a, s), second, s, a, 2, True) for s in (1, 3)],
                sends=[exchange(a, 2)],
            )

        def settled(dy):
            needs = []
            for dz in range(RING):
                a, b = (dz, dy) if first == "z" else (dy, dz)

                def refs(a=a, b=b):
                    return held(a, b, other=True), env.partner

                needs.append(((number, "x", a, b), refs))
            return needs

        return settled

    settled = [gather(("g", i), *part) for i, part in enumerate(GATHER_PARTS)]

    chunk_bytes = 2 * block * rows * 2

    def turn_refs(i):
        def refs():
            span = pl.ds(2 * env.chunk(*CHUNKS[i]), 2)
            return (
                env.turned.at[span, 1 - env.core],
                env.turned_other.at[span],
                env.partner,
            )

        return refs

    def turn_need(i):
        def refs():
            return turn_refs(i)()[1], env.partner

        return ("t", i), refs

    add(
        "cot",
        lambda: env.start_rest(),
        0.4,
        0,
        sends=[
            (
                "cot",
                "c",
                rows * WIDTH * 2,
                lambda: (env.cotangent, env.cot.at[1], env.partner),
            )
        ],
    )
    add("square", lambda: env.square(), 2.5, 2, after=["cot"])
    for i in range(len(CHUNKS)):
        add(
            ("turn", i),
            lambda i=i: env.turn(env.chunk(*CHUNKS[i])),
            0.4,
            0.5,
            after=["square"] + ([("turn", i - 1)] if i else []),
            sends=[(("t", i), "c", chunk_bytes, turn_refs(i))],
        )
        needs = [turn_need(i)]
        if i == 0:
            needs.append(("cot", lambda: (env.cot.at[1], env.partner)))
        add(
            ("product", i),
            lambda i=i: env.multiply(env.chunk(*CHUNKS[i])),
            0.15,
            2.5,
            needs=needs,
            after=[("product", i - 1)] if i else [],
        )

    def scatter(number, lo, hi, first):
        size = hi - lo
        second = "y" if first == "z" else "z"
        halves = {1: pl.ds(0, size // 2), 3: pl.ds(size // 2, size // 2)}
        index = {1: 0, 3: 1}
        start = {1: lo, 3: lo + size // 2}
        whole_size, half_size = size * WIDTH * 2, size * WIDTH
        bf16, f32 = jnp.bfloat16, jnp.float32

        def offset(a, b):
            return (b, a) if first == "z" else (a, b)

        def target(axis, s):
            return env.device(0, s) if axis == "z" else env.device(s, 0)

        def mine(a, b, s=None):
            span = pl.ds(lo, size) if s is None else pl.ds(start[s], size // 2)
            return env.part[env.chip[offset(a, b)], span, :]

        def bufs():
            return env.scatter[number[1]]

        def far_refs(b, s):
            r = bufs()
            return (
                r.far_out.at[b, halves[s]],
                r.far_in.at[b, halves[s]],
                target(first, s),
            )

        def near_refs(b, s):
            r = bufs()
            return r.near_out.at[index[s], b], r.near_in.at[index[s], b], target(first, s)

        def far2_refs(s):
            r = bufs()
            return r.far2_out.at[halves[s]], r.far2_in.at[halves[s]], target(second, s)

        def near2_refs(s):
            r = bufs()
            return r.near2_out.at[index[s]], r.near2_in.at[index[s]], target(second, s)

        def need(key, fn, *args):
            return (number, *key), lambda: fn(*args)[1:]

        def far(b):
            for s in (1, 3):
                bufs().far_out[b, halves[s], :] = mine(2, b, s).astype(bf16)

        def near(b, s):
            r, i = bufs(), index[s]
            r.near_out[i, b, halves[OPPOSITE[s]], :] = mine(s, b, OPPOSITE[s]).astype(bf16)
            r.near_out[i, b, halves[s], :] = (
                mine(s, b, s) + r.far_in[b, halves[s], :].astype(f32)
            ).astype(bf16)

        def gathered(b):
            r = bufs()
            r.total[b] = (
                mine(0, b) + r.near_in[0, b].astype(f32) + r.near_in[1, b].astype(f32)
            )

        def far2():
            r = bufs()
            for s in (1, 3):
                r.far2_out[halves[s], :] = r.total[2, halves[s], :].astype(bf16)

        def near2(s):
            r, i, o = bufs(), index[s], halves[OPPOSITE[s]]
            r.near2_out[i, o, :] = r.total[s, o, :].astype(bf16)
            r.near2_out[i, halves[s], :] = (
                r.total[s, halves[s], :] + r.far2_in[halves[s], :].astype(f32)
            ).astype(bf16)

        def final():
            r = bufs()
            env.weight_out[pl.ds(lo, size), :] = (
                r.total[0] + r.near2_in[0].astype(f32) + r.near2_in[1].astype(f32)
            )

        for b in (2, 1, 3, 0):
            add(
                (number, "far", b),
                functools.partial(far, b),
                0.15,
                2,
                after=product(*offset(2, b)),
                sends=[
                    (
                        (number, "f", b, s),
                        first + str(s),
                        half_size,
                        functools.partial(far_refs, b, s),
                    )
                    for s in (1, 3)
                ],
            )
            for s in (1, 3):
                add(
                    (number, "near", b, s),
                    functools.partial(near, b, s),
                    0.2,
                    2,
                    needs=[need(("f", b, s), far_refs, b, s)],
                    after=product(*offset(s, b)) + [(number, "far", b)],
                    sends=[
                        (
                            (number, "n", b, s),
                            first + str(s),
                            whole_size,
                            functools.partial(near_refs, b, s),
                        )
                    ],
                )
            add(
                (number, "sum", b),
                functools.partial(gathered, b),
                0.2,
                2,
                needs=[need(("n", b, s), near_refs, b, s) for s in (1, 3)],
                after=product(*offset(0, b)),
            )
        add(
            (number, "far2"),
            far2,
            0.1,
            2,
            after=[(number, "sum", 2)],
            sends=[
                (
                    (number, "f2", s),
                    second + str(s),
                    half_size,
                    functools.partial(far2_refs, s),
                )
                for s in (1, 3)
            ],
        )
        for s in (1, 3):
            add(
                (number, "near2", s),
                functools.partial(near2, s),
                0.2,
                2,
                needs=[need(("f2", s), far2_refs, s)],
                after=[(number, "sum", s)],
                sends=[
                    (
                        (number, "n2", s),
                        second + str(s),
                        whole_size,
                        functools.partial(near2_refs, s),
                    )
                ],
            )
        add(
            (number, "final"),
            final,
            0.3,
            2,
            needs=[need(("n2", s), near2_refs, s) for s in (1, 3)],
            after=[(number, "sum", 0)],
        )

    for i, part in enumerate(SCATTER_PARTS):
        scatter(("s", i), *part)

    def x_refs(d):
        return env.x_in.at[env.x], env.x_in.at[env.x], env.beside_x(d)

    def x_need(d):
        return ("ox", d), lambda: (
            env.x_in.at[lax.rem(env.x + RING - d, RING)],
            env.beside_x(d),
        )

    add(
        "outer",
        lambda: env.differ(),
        0.5,
        2.2,
        after=["square"],
        sends=[
            (("ox", d), "x" + str(d), 65536, functools.partial(x_refs, d)) for d in (1, 2, 3)
        ],
    )
    add(
        "outer2",
        lambda: env.add_x(),
        0.5,
        4,
        needs=[x_need(d) for d in (1, 2, 3)],
        sends=[("oz", "z1", 65536, lambda: (env.z_out, env.z_in, env.beside_low))],
    )
    add(
        "outer3",
        lambda: env.update(),
        0.8,
        4,
        needs=[("oz", lambda: (env.z_in, env.beside_low))],
    )

    add("own", lambda: env.own_copy.wait(), 0.0, 2, after=["square"])
    gain_bytes = features // RING * 4
    for dy in (0, 1, 3, 2):
        add(
            ("project", dy),
            functools.partial(lambda dy: env.project(dy), dy),
            1.0,
            2.8,
            needs=[n for fn in settled for n in fn(dy)],
            after=["own"],
            sends=[
                (
                    ("gc", dy),
                    "c",
                    gain_bytes,
                    lambda dy=dy: (env.gain_own.at[dy], env.gain_core.at[dy], env.partner),
                )
            ],
        )
        if dy:
            sends = [
                (
                    ("gy", dy),
                    "y" + str(dy) if dy != 2 else "y1",
                    gain_bytes,
                    lambda dy=dy: (
                        env.gain_chip.at[dy],
                        env.gain_y.at[dy],
                        env.device(dy, 0),
                    ),
                )
            ]
        else:
            sends = []
        add(
            ("gain", dy),
            functools.partial(lambda dy: env.gain_chip_sum(dy), dy),
            0.1,
            1,
            needs=[
                (("gc", dy), lambda dy=dy: (env.gain_core.at[dy], env.partner))
            ],
            after=[("project", dy)],
            sends=sends,
        )
    add(
        "gain y",
        lambda: env.gain_y_sum(),
        0.1,
        1,
        needs=[
            (("gy", d), lambda d=d: (env.gain_y.at[d], env.device(d, 0))) for d in (1, 2, 3)
        ],
        after=[("gain", 0)],
        sends=[
            (
                ("gz", d),
                "z" + str(d) if d != 2 else "z1",
                gain_bytes,
                lambda d=d: (env.gain_z.at[0], env.gain_z.at[d], env.device(0, d)),
            )
            for d in (1, 2, 3)
        ],
    )
    add(
        "gain z",
        lambda: env.gain_z_sum(),
        0.2,
        3,
        needs=[
            (("gz", d), lambda d=d: (env.gain_z.at[d], env.device(0, d))) for d in (1, 2, 3)
        ],
    )
    add(
        "finish",
        lambda: env.finish(),
        2.0,
        2.9,
        after=[("project", dy) for dy in range(RING)],
    )
    return events


def kernel(
    plan,
    tokens,
    gain_all,
    weight,
    cotangent,
    replica_part,
    anchor,
    velocity,
    chosen,
    token_out,
    weight_out,
    gain_out,
    param_out,
    momentum_out,
    gain,
    turned,
    turned_other,
    cot,
    full,
    part,
    scaled,
    inverse,
    projected,
    gain_own,
    gain_core,
    gain_chip,
    gain_y,
    gain_z,
    replica_in,
    anchor_in,
    velocity_in,
    x_in,
    z_out,
    z_in,
    *rest,
):
    buffers, (send_sem, recv_sem, local_sem) = rest[:-3], rest[-3:]
    rows, features = token_out.shape
    block = weight.shape[0]
    f32, bf16 = jnp.float32, jnp.bfloat16
    tok = token_out

    worker = lax.axis_index("worker")
    place = lax.axis_index("fsdp")
    core = lax.rem(place, 2)
    z = lax.rem(place // 2, RING)
    y = place // (2 * RING)
    x, low = worker // 2, lax.rem(worker, 2)

    env = types.SimpleNamespace(
        core=core,
        x=x,
        weight=weight,
        cotangent=cotangent,
        cot=cot,
        turned=turned,
        turned_other=turned_other,
        part=part,
        x_in=x_in,
        z_out=z_out,
        z_in=z_in,
        weight_out=weight_out,
        gain_own=gain_own,
        gain_core=gain_core,
        gain_chip=gain_chip,
        gain_y=gain_y,
        gain_z=gain_z,
    )
    env.chip = {
        (dy, dz): lax.rem(y + dy, RING) * RING + lax.rem(z + dz, RING)
        for dy in range(RING)
        for dz in range(RING)
    }
    env.device = lambda dy, dz: {"fsdp": 2 * env.chip[dy, dz] + core}
    env.partner = {"fsdp": place + 1 - 2 * core}
    env.beside_x = lambda d: {"worker": lax.rem(x + d, RING) * 2 + low}
    env.beside_low = {"worker": x * 2 + 1 - low}
    env.chunk = lambda dy, far: lax.rem(y + dy, RING) * 2 + (
        1 - z // 2 if far else z // 2
    )
    names = ["far_out", "far_in", "near_out", "near_in"]
    names += ["far2_out", "far2_in", "near2_out", "near2_in", "total"]
    env.scatter = [
        types.SimpleNamespace(**dict(zip(names, buffers[9 * i : 9 * i + 9])))
        for i in range(len(SCATTER_PARTS))
    ]

    def slot(dy, dz, which, lo, hi):
        start = (2 * env.chip[dy, dz] + which) * block + lo
        return full.at[pl.ds(pl.multiple_of(start, 16), hi - lo)]

    env.slot = slot

    half_rows = rows // 2
    token_copies = []
    for i in range(2):
        span = pl.ds(i * half_rows, half_rows)
        token_copies.append(
            pltpu.make_async_copy(tokens.at[span], tok.at[span], local_sem.at[i])
        )
    cot_copy = pltpu.make_async_copy(cotangent, cot.at[0], local_sem.at[2])
    gain_copy = pltpu.make_async_copy(gain_all, gain, local_sem.at[7])
    own = pl.ds(pl.multiple_of(place * block, 16), block)
    env.own_copy = pltpu.make_async_copy(weight, full.at[own], local_sem.at[3])
    fragment_copies = [
        pltpu.make_async_copy(src, dst, local_sem.at[4 + i])
        for i, (src, dst) in enumerate(
            ((replica_part, replica_in), (anchor, anchor_in), (velocity, velocity_in))
        )
    ]
    greeted = [env.partner, env.beside_low]
    greeted += [env.beside_x(d) for d in (1, 2, 3)]
    greeted += [env.device(d, 0) for d in (1, 2, 3)]
    greeted += [env.device(0, d) for d in (1, 2, 3)]
    barrier = pltpu.get_barrier_semaphore()
    for target in greeted:
        pl.semaphore_signal(barrier, inc=1, device_id=target, device_id_type=MESH)
    for c in token_copies:
        c.start()
    pl.semaphore_wait(barrier, len(greeted))

    def start_rest():
        for c in (gain_copy, cot_copy, env.own_copy, *fragment_copies):
            c.start()

    def square():
        projected[...] = jnp.zeros_like(projected)
        for c in (gain_copy, cot_copy):
            c.wait()
        for i in range(2):
            token_copies[i].wait()
            here = pl.ds(i * half_rows, half_rows)

            def step(j, total):
                wide = tok[here, pl.ds(pl.multiple_of(j * 256, 128), 256)].astype(f32)
                wide = wide * wide
                return total + wide[:, :128] + wide[:, 128:]

            total = lax.fori_loop(
                0, features // 256, step, jnp.zeros((half_rows, 128), f32)
            )
            inv = lax.rsqrt(jnp.sum(total, axis=1, keepdims=True) / features + EPSILON)
            inverse[here, :] = jnp.broadcast_to(inv, (half_rows, 128))

    def turn(j):
        width = 4 * block
        cols = pl.ds(pl.multiple_of(j * width, 128), width)
        for i in range(2):
            here = pl.ds(i * half_rows, half_rows)
            inv = inverse[here, 0:1]
            normed = (tok[here, cols].astype(f32) * inv * gain[:, cols]).astype(bf16)
            flipped = normed.T
            for b in range(4):
                turned[2 * j + b // 2, b % 2, :, here] = flipped[
                    b * block : (b + 1) * block
                ]
        for k in range(2):
            part[2 * j + k] = jnp.dot(
                turned[2 * j + k, core], cot[0], preferred_element_type=f32
            )

    def multiply(j):
        for k in range(2):
            part[2 * j + k] += jnp.dot(
                turned_other[2 * j + k], cot[1], preferred_element_type=f32
            )

    span = features // RING
    width = span // 2

    def project(dy):
        start = pl.multiple_of(lax.rem(y + dy, RING) * span, 128)

        @pl.loop(0, 2)
        def _(i):
            here = pl.ds(pl.multiple_of(start + i * width, 128), width)
            d = lax.dot_general(cot[0], full[here, :], NT, preferred_element_type=f32)
            scale = gain[:, here]
            scaled[:, here] = d * scale
            both = d * tok[:, here].astype(f32)
            with_gain = both * scale
            total = with_gain[:, :128]
            for k in range(1, width // 128):
                total = total + with_gain[:, k * 128 : (k + 1) * 128]
            projected[...] += total
            inv = inverse[...]
            for k in range(width // 128):
                cols = pl.ds(pl.multiple_of(i * width + k * 128, 128), 128)
                gain_own[dy, :, cols] = jnp.sum(
                    both[:, k * 128 : (k + 1) * 128] * inv, axis=0, keepdims=True
                )

    def finish():
        step = 64

        @pl.loop(0, rows // step)
        def _(i):
            here = pl.ds(pl.multiple_of(i * step, step), step)
            inv = inverse[here, 0:1]
            mean = jnp.sum(projected[here, :], axis=1, keepdims=True) / features
            back = inv * inv * inv * mean

            for j in range(features // 1024):
                cols = pl.ds(j * 1024, 1024)
                wide = tok[here, cols].astype(f32)
                tok[here, cols] = (inv * scaled[here, cols] - wide * back).astype(bf16)

    def gain_chip_sum(dy):
        total = gain_own[dy] + gain_core[dy]
        if dy:
            gain_chip[dy] = total
        else:
            gain_y[0] = total

    def gain_y_sum():
        gain_z[0] = gain_y[0] + gain_y[1] + gain_y[2] + gain_y[3]

    def gain_z_sum():
        total = gain_z[0] + gain_z[1] + gain_z[2] + gain_z[3]
        which = 2 * z + core
        chosen_part = total[:, :block]
        for i in range(1, 2 * RING):
            chosen_part = jnp.where(
                which == i, total[:, i * block : (i + 1) * block], chosen_part
            )
        gain_out[...] = chosen_part

    def differ():
        for c in fragment_copies:
            c.wait()
        index = chosen[0]
        x_in[x] = anchor_in[pl.ds(index, 1), :] - replica_in[pl.ds(index, 1), :]

    def add_x():
        z_out[...] = x_in[0] + x_in[1] + x_in[2] + x_in[3]

    def update():
        index = chosen[0]
        pseudo = (z_out[...] + z_in[...]) / 8
        momentum = MOMENTUM * velocity_in[pl.ds(index, 1), :] + pseudo
        momentum_out[...] = momentum
        param_out[...] = anchor_in[pl.ds(index, 1), :] - OUTER_RATE * (
            pseudo + MOMENTUM * momentum
        )

    for fn in (
        start_rest,
        square,
        turn,
        multiply,
        project,
        finish,
        gain_chip_sum,
        gain_y_sum,
        gain_z_sum,
        differ,
        add_x,
        update,
    ):
        setattr(env, fn.__name__, fn)

    order = plan(env)
    numbers = {}
    for e in order:
        for key, _, _, _ in e.sends:
            numbers[key] = len(numbers)

    def copy(key, src, dst, target):
        return pltpu.make_async_remote_copy(
            src_ref=src,
            dst_ref=dst,
            send_sem=send_sem.at[numbers[key]],
            recv_sem=recv_sem.at[numbers[key]],
            device_id=target,
            device_id_type=MESH,
        )

    sent = []
    for e in order:
        for key, refs in e.needs:
            dst, target = refs()
            copy(key, dst, dst, target).wait_recv()
        e.body()
        for key, _, _, refs in e.sends:
            c = copy(key, *refs())
            c.start()
            sent.append(c)
    for c in sent:
        c.wait_send()


def write_out(*refs):
    count = len(refs) // 2
    sem = refs[-1]
    copies = [
        pltpu.make_async_copy(refs[i], refs[count + i], sem.at[i]) for i in range(count)
    ]
    for c in copies:
        c.start()
    for c in copies:
        c.wait()


def local(
    tokens,
    norm_gain,
    value_weight,
    value_cotangent,
    local_fragments,
    global_fragments,
    outer_velocity,
    fragment_index,
):
    _, rows, features = tokens.shape
    _, block, values = value_weight.shape
    blocks = RING * RING
    fragments, length = global_fragments.shape
    span = features // RING
    vmem = pltpu.VMEM
    bf16, f32 = jnp.bfloat16, jnp.float32

    def plan(env):
        events = build(env, rows, features, block)
        return [events[i] for i in ORDER]

    sems = sum(len(e.sends) for e in plan(None))
    scratch = [
        vmem((1, features), f32),
        vmem((blocks, 2, block, rows), bf16),
        vmem((blocks, block, rows), bf16),
        vmem((2, rows, values), bf16),
        vmem((features, values), bf16),
        vmem((blocks, block, values), f32),
        vmem((rows, features), f32),
        vmem((rows, 128), f32),
        vmem((rows, 128), f32),
        vmem((RING, 1, span), f32),
        vmem((RING, 1, span), f32),
        vmem((RING, 1, span), f32),
        vmem((RING, 1, span), f32),
        vmem((RING, 1, span), f32),
        vmem((fragments, length), f32),
        vmem((fragments, length), f32),
        vmem((fragments, length), f32),
        vmem((RING, 1, length), f32),
        vmem((1, length), f32),
        vmem((1, length), f32),
    ]
    for lo, hi, _ in SCATTER_PARTS:
        size = hi - lo
        scratch += [
            vmem((RING, size, values), bf16),
            vmem((RING, size, values), bf16),
            vmem((2, RING, size, values), bf16),
            vmem((2, RING, size, values), bf16),
            vmem((size, values), bf16),
            vmem((size, values), bf16),
            vmem((2, size, values), bf16),
            vmem((2, size, values), bf16),
            vmem((RING, size, values), f32),
        ]
    scratch += [
        pltpu.SemaphoreType.DMA((sems,)),
        pltpu.SemaphoreType.DMA((sems,)),
        pltpu.SemaphoreType.DMA((8,)),
    ]
    in_vmem = pl.BlockSpec(memory_space=pltpu.VMEM)
    in_hbm = pl.BlockSpec(memory_space=pltpu.HBM)
    shapes = [
        ((rows, features), bf16),
        ((block, values), f32),
        ((1, block), f32),
        ((1, length), f32),
        ((1, length), f32),
    ]
    keep = functools.partial(pltpu.with_memory_space_constraint, memory_space=pltpu.HBM)
    results = pl.pallas_call(
        functools.partial(kernel, plan),
        out_shape=[vmem(*s) for s in shapes],
        in_specs=[in_hbm] * 7 + [pl.BlockSpec(memory_space=pltpu.SMEM)],
        out_specs=[in_vmem] * len(shapes),
        scratch_shapes=scratch,
        compiler_params=pltpu.CompilerParams(
            collective_id=0, has_side_effects=True, vmem_limit_bytes=42 * 2**20
        ),
        cost_estimate=pl.CostEstimate(
            flops=4 * rows * features * values, bytes_accessed=2**24, transcendentals=0
        ),
    )(
        keep(tokens[0]),
        keep(norm_gain),
        keep(value_weight[0]),
        keep(value_cotangent[0]),
        keep(local_fragments[0]),
        keep(global_fragments),
        keep(outer_velocity),
        fragment_index,
    )
    results = [pltpu.with_memory_space_constraint(r, pltpu.VMEM) for r in results]
    token_grad, weight_grad, gain_grad, param, momentum = pl.pallas_call(
        write_out,
        out_shape=[jax.ShapeDtypeStruct(*s) for s in shapes],
        in_specs=[in_vmem] * len(shapes),
        out_specs=[in_hbm] * len(shapes),
        scratch_shapes=[pltpu.SemaphoreType.DMA((len(shapes),))],
        compiler_params=pltpu.CompilerParams(vmem_limit_bytes=2**20),
    )(*results)
    return (
        token_grad[None],
        weight_grad[None],
        gain_grad,
        param.reshape(-1),
        momentum.reshape(-1),
    )


def solution(mesh):
    placed = (
        P("worker", "fsdp", None),
        P("worker", None),
        P("worker", "fsdp", None),
        P("worker", "fsdp", None),
        P("worker", None, "fsdp"),
        P(None, "fsdp"),
        P(None, "fsdp"),
        P(),
    )
    return jax.shard_map(
        local,
        mesh=mesh,
        in_specs=placed,
        out_specs=(
            P("worker", "fsdp", None),
            P("worker", "fsdp", None),
            P("worker", "fsdp"),
            P("fsdp"),
            P("fsdp"),
        ),
        check_vma=False,
    )
```

```python
import functools
import types

import jax
import jax.numpy as jnp
from jax import lax
from jax.experimental import pallas as pl
from jax.experimental.pallas import tpu as pltpu
from jax.sharding import PartitionSpec as P

EPSILON = 1e-05
MOMENTUM = 0.9
OUTER_RATE = 0.7
MESH = pl.DeviceIdType.MESH
RING = 4
NT = (((1,), (1,)), ((), ()))
GATHER_PARTS = ((0, 224, "z"),)
SCATTER_PARTS = ((0, 64, "y"), (64, 144, "y"), (144, 224, "z"))
WIDTH = 512
LAG = 12
PIECES = 4
ORDER = (
    0, 16, 17, 18, 20, 22, 24, 19, 34, 54, 21, 78, 23, 94, 25, 58, 82, 38, 42, 26, 28, 4, 5, 35,
    62, 98, 27, 29, 39, 36, 55, 95, 56, 2, 1, 30, 31, 57, 84, 79, 74, 3, 32, 70, 40, 11, 96, 37,
    10, 86, 50, 6, 7, 83, 75, 8, 76, 99, 14, 97, 64, 33, 87, 13, 88, 63, 43, 101, 102, 41, 80,
    51, 12, 85, 60, 59, 103, 46, 44, 66, 9, 15, 65, 72, 105, 77, 90, 100, 61, 71, 106, 104, 48,
    47, 45, 52, 67, 68, 81, 92, 89, 91, 107, 49, 109, 69, 73, 53, 108, 93,
)
OPPOSITE = {1: 3, 3: 1, 2: 2}
CHUNKS = ((2, 1), (1, 1), (3, 1), (2, 0), (0, 1), (1, 0), (3, 0), (0, 0))


class Event:
    def __init__(self, name, body, cost, rank, needs=(), after=(), sends=()):
        self.name, self.body, self.cost, self.rank = name, body, cost, rank
        self.needs, self.after, self.sends = list(needs), list(after), list(sends)


def build(env, rows, features, block):
    events = []

    def add(name, *args, **kw):
        events.append(Event(name, *args, **kw))

    def nothing():
        pass

    chunk_of = {c: i for i, c in enumerate(CHUNKS)}

    def product(dy, dz):
        sides = {0: (0,), 2: (1,), 1: (0, 1), 3: (0, 1)}[dz]
        return [("product", chunk_of[dy, s]) for s in sides]

    def gather(number, lo, hi, first):
        mid = lo + (hi - lo) // 32 * 16
        halves = {1: (lo, mid), 3: (mid, hi)}
        second = "y" if first == "z" else "z"
        full_size = (hi - lo) * WIDTH * 2
        half_size = {1: (mid - lo) * WIDTH * 2, 3: (hi - mid) * WIDTH * 2}

        def offset(a, b):
            return (b, a) if first == "z" else (a, b)

        def target(axis, s):
            return env.device(0, s) if axis == "z" else env.device(s, 0)

        def held(a, b, span=(lo, hi), other=False):
            which = 1 - env.core if other else env.core
            return env.slot(*offset(a, b), which, *span)

        def whole(key, axis, s, a, b, own=False):
            def refs():
                here = held(a, b)
                src = env.weight.at[pl.ds(lo, hi - lo)] if own else here
                return src, here, target(axis, s)

            return (number, *key), axis + str(s), full_size, refs

        def half(key, axis, s, a, b):
            def refs():
                here = held(a, b, halves[s])
                return here, here, target(axis, s)

            return (number, *key), axis + str(s), half_size[s], refs

        def exchange(a, b, own=False):
            def refs():
                here = held(a, b)
                src = env.weight.at[pl.ds(lo, hi - lo)] if own else here
                return src, here, env.partner

            return (number, "x", a, b), "c", full_size, refs

        def need(key, axis, s, a, b, part=False):
            def refs():
                return held(a, b, halves[s] if part else (lo, hi)), target(axis, s)

            return (number, *key), refs

        def spread(a, own=False):
            return [whole(("b", a, s), second, s, a, 0, own) for s in (1, 3)]

        add(
            (number, "begin"),
            nothing,
            0.1,
            0,
            sends=[whole(("a", s), first, s, 0, 0, True) for s in (1, 3)]
            + spread(0, True)
            + [exchange(0, 0, True)],
        )
        for s in (1, 3):
            a = OPPOSITE[s]
            add(
                (number, "first", s),
                nothing,
                0.1,
                1,
                needs=[need(("a", s), first, s, a, 0)],
                sends=[half(("af", s), first, s, a, 0), *spread(a), exchange(a, 0)],
            )
        add(
            (number, "first", 2),
            nothing,
            0.1,
            1,
            needs=[need(("af", s), first, s, 2, 0, True) for s in (1, 3)],
            sends=[*spread(2), exchange(2, 0)],
        )
        for a in (0, 3, 1, 2):
            for s in (1, 3):
                b = OPPOSITE[s]
                add(
                    (number, "second", a, s),
                    nothing,
                    0.1,
                    1,
                    needs=[need(("b", a, s), second, s, a, b)],
                    sends=[half(("bf", a, s), second, s, a, b), exchange(a, b)],
                )
            add(
                (number, "second", a, 2),
                nothing,
                0.1,
                1,
                needs=[need(("bf", a, s), second, s, a, 2, True) for s in (1, 3)],
                sends=[exchange(a, 2)],
            )

        def settled(dy):
            needs = []
            for dz in range(RING):
                a, b = (dz, dy) if first == "z" else (dy, dz)

                def refs(a=a, b=b):
                    return held(a, b, other=True), env.partner

                needs.append(((number, "x", a, b), refs))
            return needs

        return settled

    settled = [gather(("g", i), *part) for i, part in enumerate(GATHER_PARTS)]

    chunk_bytes = 2 * block * rows * 2

    def turn_refs(i):
        def refs():
            span = pl.ds(2 * env.chunk(*CHUNKS[i]), 2)
            return (
                env.turned.at[span, 1 - env.core],
                env.turned_other.at[span],
                env.partner,
            )

        return refs

    def turn_need(i):
        def refs():
            return turn_refs(i)()[1], env.partner

        return ("t", i), refs

    add(
        "cot",
        lambda: env.start_rest(),
        0.4,
        0,
        sends=[
            (
                "cot",
                "c",
                rows * WIDTH * 2,
                lambda: (env.cotangent, env.cot.at[1], env.partner),
            )
        ],
    )
    add("square", lambda: env.square(), 2.5, 2, after=["cot"])
    for i in range(len(CHUNKS)):
        add(
            ("turn", i),
            lambda i=i: env.turn(env.chunk(*CHUNKS[i])),
            0.4,
            0.5,
            after=["square"] + ([("turn", i - 1)] if i else []),
            sends=[(("t", i), "c", chunk_bytes, turn_refs(i))],
        )
        needs = [turn_need(i)]
        if i == 0:
            needs.append(("cot", lambda: (env.cot.at[1], env.partner)))
        add(
            ("product", i),
            lambda i=i: env.multiply(env.chunk(*CHUNKS[i])),
            0.15,
            2.5,
            needs=needs,
            after=[("product", i - 1)] if i else [],
        )

    def scatter(number, lo, hi, first):
        size = hi - lo
        second = "y" if first == "z" else "z"
        mid = size // 32 * 16
        halves = {1: pl.ds(0, mid), 3: pl.ds(mid, size - mid)}
        index = {1: 0, 3: 1}
        spans = {1: pl.ds(lo, mid), 3: pl.ds(lo + mid, size - mid)}
        whole_size = size * WIDTH * 2
        half_size = {1: mid * WIDTH * 2, 3: (size - mid) * WIDTH * 2}
        bf16, f32 = jnp.bfloat16, jnp.float32

        def offset(a, b):
            return (b, a) if first == "z" else (a, b)

        def target(axis, s):
            return env.device(0, s) if axis == "z" else env.device(s, 0)

        def mine(a, b, s=None):
            span = pl.ds(lo, size) if s is None else spans[s]
            return env.part[env.chip[offset(a, b)], span, :]

        def bufs():
            return env.scatter[number[1]]

        def far_refs(b, s):
            r = bufs()
            return (
                r.far_out.at[b, halves[s]],
                r.far_in.at[b, halves[s]],
                target(first, s),
            )

        def near_refs(b, s):
            r = bufs()
            return r.near_out.at[index[s], b], r.near_in.at[index[s], b], target(first, s)

        def far2_refs(s):
            r = bufs()
            return r.far2_out.at[halves[s]], r.far2_in.at[halves[s]], target(second, s)

        def near2_refs(s):
            r = bufs()
            return r.near2_out.at[index[s]], r.near2_in.at[index[s]], target(second, s)

        def need(key, fn, *args):
            return (number, *key), lambda: fn(*args)[1:]

        def far(b):
            for s in (1, 3):
                bufs().far_out[b, halves[s], :] = mine(2, b, s).astype(bf16)

        def near(b, s):
            r, i = bufs(), index[s]
            r.near_out[i, b, halves[OPPOSITE[s]], :] = mine(s, b, OPPOSITE[s]).astype(bf16)
            r.near_out[i, b, halves[s], :] = (
                mine(s, b, s) + r.far_in[b, halves[s], :].astype(f32)
            ).astype(bf16)

        def gathered(b):
            r = bufs()
            r.total[b] = (
                mine(0, b) + r.near_in[0, b].astype(f32) + r.near_in[1, b].astype(f32)
            )

        def far2():
            r = bufs()
            for s in (1, 3):
                r.far2_out[halves[s], :] = r.total[2, halves[s], :].astype(bf16)

        def near2(s):
            r, i, o = bufs(), index[s], halves[OPPOSITE[s]]
            r.near2_out[i, o, :] = r.total[s, o, :].astype(bf16)
            r.near2_out[i, halves[s], :] = (
                r.total[s, halves[s], :] + r.far2_in[halves[s], :].astype(f32)
            ).astype(bf16)

        def final():
            r = bufs()
            env.weight_out[pl.ds(lo, size), :] = (
                r.total[0] + r.near2_in[0].astype(f32) + r.near2_in[1].astype(f32)
            )

        for b in (2, 1, 3, 0):
            add(
                (number, "far", b),
                functools.partial(far, b),
                0.15,
                2,
                after=product(*offset(2, b)),
                sends=[
                    (
                        (number, "f", b, s),
                        first + str(s),
                        half_size[s],
                        functools.partial(far_refs, b, s),
                    )
                    for s in (1, 3)
                ],
            )
            for s in (1, 3):
                add(
                    (number, "near", b, s),
                    functools.partial(near, b, s),
                    0.12,
                    2,
                    needs=[need(("f", b, s), far_refs, b, s)],
                    after=product(*offset(s, b)) + [(number, "far", b)],
                    sends=[
                        (
                            (number, "n", b, s),
                            first + str(s),
                            whole_size,
                            functools.partial(near_refs, b, s),
                        )
                    ],
                )
            add(
                (number, "sum", b),
                functools.partial(gathered, b),
                0.2,
                2,
                needs=[need(("n", b, s), near_refs, b, s) for s in (1, 3)],
                after=product(*offset(0, b)),
            )
        add(
            (number, "far2"),
            far2,
            0.1,
            2,
            after=[(number, "sum", 2)],
            sends=[
                (
                    (number, "f2", s),
                    second + str(s),
                    half_size[s],
                    functools.partial(far2_refs, s),
                )
                for s in (1, 3)
            ],
        )
        for s in (1, 3):
            add(
                (number, "near2", s),
                functools.partial(near2, s),
                0.2,
                2,
                needs=[need(("f2", s), far2_refs, s)],
                after=[(number, "sum", s)],
                sends=[
                    (
                        (number, "n2", s),
                        second + str(s),
                        whole_size,
                        functools.partial(near2_refs, s),
                    )
                ],
            )
        add(
            (number, "final"),
            final,
            0.3,
            2,
            needs=[need(("n2", s), near2_refs, s) for s in (1, 3)],
            after=[(number, "sum", 0)],
        )

    for i, part in enumerate(SCATTER_PARTS):
        scatter(("s", i), *part)

    def x_from(d):
        return lax.rem(env.x + RING - d, RING)

    def x_refs(d):
        return env.quarter(lax.rem(env.x + d, RING)), env.x_in.at[env.x], env.beside_x(d)

    def x_need(d):
        return ("ox", d), lambda: (env.x_in.at[x_from(d)], env.beside_x(d))

    def all_refs(d):
        return env.total.at[env.x], env.total.at[env.x], env.beside_x(d)

    def all_need(d):
        return ("oa", d), lambda: (env.total.at[x_from(d)], env.beside_x(d))

    def to_x(key, refs):
        return [
            ((key, d), "x" + str(d), 16384, functools.partial(refs, d)) for d in (1, 2, 3)
        ]

    add(
        "outer",
        lambda: env.differ(),
        0.5,
        2.2,
        after=["square"],
        sends=to_x("ox", x_refs),
    )
    add(
        "outer2",
        lambda: env.add_x(),
        0.2,
        4,
        needs=[x_need(d) for d in (1, 2, 3)],
        sends=[("oz", "z1", 8192, lambda: (env.z_out, env.z_in, env.beside_low))],
    )
    add(
        "outer3",
        lambda: env.add_z(),
        0.1,
        4,
        needs=[("oz", lambda: (env.z_in, env.beside_low))],
        sends=to_x("oa", all_refs),
    )
    add(
        "outer4",
        lambda: env.update(),
        0.6,
        4,
        needs=[all_need(d) for d in (1, 2, 3)],
    )

    add("own", lambda: env.own_copy.wait(), 0.0, 2, after=["square"])
    gain_bytes = features // RING * 4
    for dy in (0, 1, 3, 2):
        add(
            ("project", dy),
            functools.partial(lambda dy: env.project(dy), dy),
            1.0,
            2.8,
            needs=[n for fn in settled for n in fn(dy)],
            after=["own"],
            sends=[
                (
                    ("gc", dy),
                    "c",
                    gain_bytes,
                    lambda dy=dy: (env.gain_own.at[dy], env.gain_core.at[dy], env.partner),
                )
            ],
        )
        if dy:
            sends = [
                (
                    ("gy", dy),
                    "y" + str(dy) if dy != 2 else "y1",
                    gain_bytes,
                    lambda dy=dy: (
                        env.gain_chip.at[dy],
                        env.gain_y.at[dy],
                        env.device(dy, 0),
                    ),
                )
            ]
        else:
            sends = []
        add(
            ("gain", dy),
            functools.partial(lambda dy: env.gain_chip_sum(dy), dy),
            0.1,
            1,
            needs=[
                (("gc", dy), lambda dy=dy: (env.gain_core.at[dy], env.partner))
            ],
            after=[("project", dy)],
            sends=sends,
        )
    add(
        "gain y",
        lambda: env.gain_y_sum(),
        0.1,
        1,
        needs=[
            (("gy", d), lambda d=d: (env.gain_y.at[d], env.device(d, 0))) for d in (1, 2, 3)
        ],
        after=[("gain", 0)],
        sends=[
            (
                ("gz", d),
                "z" + str(d) if d != 2 else "z1",
                gain_bytes,
                lambda d=d: (env.gain_z.at[0], env.gain_z.at[d], env.device(0, d)),
            )
            for d in (1, 2, 3)
        ],
    )
    add(
        "gain z",
        lambda: env.gain_z_sum(),
        0.2,
        3,
        needs=[
            (("gz", d), lambda d=d: (env.gain_z.at[d], env.device(0, d))) for d in (1, 2, 3)
        ],
    )
    add(
        "finish",
        lambda: env.finish(),
        2.0,
        2.9,
        after=[("project", dy) for dy in range(RING)],
    )
    return events


def kernel(
    plan,
    tokens,
    gain_all,
    weight,
    cotangent,
    replica_part,
    anchor,
    velocity,
    chosen,
    token_out,
    weight_out,
    gain_out,
    param_out,
    momentum_out,
    gain,
    turned,
    turned_other,
    cot,
    full,
    part,
    scaled,
    inverse,
    projected,
    gain_own,
    gain_core,
    gain_chip,
    gain_y,
    gain_z,
    replica_in,
    anchor_in,
    velocity_in,
    difference,
    x_in,
    z_out,
    z_in,
    total,
    *rest,
):
    buffers, (send_sem, recv_sem, local_sem) = rest[:-3], rest[-3:]
    rows, features = token_out.shape
    block = weight.shape[0]
    f32, bf16 = jnp.float32, jnp.bfloat16
    tok = token_out

    worker = lax.axis_index("worker")
    place = lax.axis_index("fsdp")
    core = lax.rem(place, 2)
    z = lax.rem(place // 2, RING)
    y = place // (2 * RING)
    x, low = worker // 2, lax.rem(worker, 2)

    env = types.SimpleNamespace(
        core=core,
        x=x,
        weight=weight,
        cotangent=cotangent,
        cot=cot,
        turned=turned,
        turned_other=turned_other,
        part=part,
        x_in=x_in,
        z_out=z_out,
        z_in=z_in,
        total=total,
        weight_out=weight_out,
        gain_own=gain_own,
        gain_core=gain_core,
        gain_chip=gain_chip,
        gain_y=gain_y,
        gain_z=gain_z,
    )
    env.chip = {
        (dy, dz): lax.rem(y + dy, RING) * RING + lax.rem(z + dz, RING)
        for dy in range(RING)
        for dz in range(RING)
    }
    env.device = lambda dy, dz: {"fsdp": 2 * env.chip[dy, dz] + core}
    env.partner = {"fsdp": place + 1 - 2 * core}
    env.beside_x = lambda d: {"worker": lax.rem(x + d, RING) * 2 + low}
    env.beside_low = {"worker": x * 2 + 1 - low}
    env.chunk = lambda dy, far: lax.rem(y + dy, RING) * 2 + (
        1 - z // 2 if far else z // 2
    )
    names = ["far_out", "far_in", "near_out", "near_in"]
    names += ["far2_out", "far2_in", "near2_out", "near2_in", "total"]
    env.scatter = [
        types.SimpleNamespace(**dict(zip(names, buffers[9 * i : 9 * i + 9])))
        for i in range(len(SCATTER_PARTS))
    ]

    def slot(dy, dz, which, lo, hi):
        start = (2 * env.chip[dy, dz] + which) * block + lo
        return full.at[pl.ds(pl.multiple_of(start, 16), hi - lo)]

    env.slot = slot

    half_rows = rows // 2
    token_copies = []
    for i in range(2):
        span = pl.ds(i * half_rows, half_rows)
        token_copies.append(
            pltpu.make_async_copy(tokens.at[span], tok.at[span], local_sem.at[i])
        )
    cot_copy = pltpu.make_async_copy(cotangent, cot.at[0], local_sem.at[2])
    gain_copy = pltpu.make_async_copy(gain_all, gain, local_sem.at[7])
    own = pl.ds(pl.multiple_of(place * block, 16), block)
    env.own_copy = pltpu.make_async_copy(weight, full.at[own], local_sem.at[3])
    fragment_copies = [
        pltpu.make_async_copy(src, dst, local_sem.at[4 + i])
        for i, (src, dst) in enumerate(
            ((replica_part, replica_in), (anchor, anchor_in), (velocity, velocity_in))
        )
    ]
    greeted = [env.device(0, d) for d in (1, 3, 2)]
    greeted += [env.device(d, 0) for d in (1, 3, 2)]
    greeted += [env.partner, env.beside_low]
    greeted += [env.beside_x(d) for d in (1, 2, 3)]
    barrier = pltpu.get_barrier_semaphore()
    for target in greeted:
        pl.semaphore_signal(barrier, inc=1, device_id=target, device_id_type=MESH)
    for c in token_copies:
        c.start()
    pl.semaphore_wait(barrier, len(greeted))

    def start_rest():
        for c in (gain_copy, cot_copy, env.own_copy, *fragment_copies):
            c.start()

    def square():
        projected[...] = jnp.zeros_like(projected)
        for c in (gain_copy, cot_copy):
            c.wait()
        for i in range(2):
            token_copies[i].wait()
            here = pl.ds(i * half_rows, half_rows)

            def step(j, total):
                wide = tok[here, pl.ds(pl.multiple_of(j * 256, 128), 256)].astype(f32)
                wide = wide * wide
                return total + wide[:, :128] + wide[:, 128:]

            total = lax.fori_loop(
                0, features // 256, step, jnp.zeros((half_rows, 128), f32)
            )
            inv = lax.rsqrt(jnp.sum(total, axis=1, keepdims=True) / features + EPSILON)
            inverse[here, :] = jnp.broadcast_to(inv, (half_rows, 128))

    def turn(j):
        width = 4 * block
        cols = pl.ds(pl.multiple_of(j * width, 128), width)
        for i in range(2):
            here = pl.ds(i * half_rows, half_rows)
            inv = inverse[here, 0:1]
            normed = (tok[here, cols].astype(f32) * inv * gain[:, cols]).astype(bf16)
            flipped = normed.T
            for b in range(4):
                turned[2 * j + b // 2, b % 2, :, here] = flipped[
                    b * block : (b + 1) * block
                ]
        for k in range(2):
            part[2 * j + k] = jnp.dot(
                turned[2 * j + k, core], cot[0], preferred_element_type=f32
            )

    def multiply(j):
        for k in range(2):
            part[2 * j + k] += jnp.dot(
                turned_other[2 * j + k], cot[1], preferred_element_type=f32
            )

    span = features // RING
    width = span // 2

    def project(dy):
        start = pl.multiple_of(lax.rem(y + dy, RING) * span, 128)

        @pl.loop(0, 2)
        def _(i):
            here = pl.ds(pl.multiple_of(start + i * width, 128), width)
            d = lax.dot_general(cot[0], full[here, :], NT, preferred_element_type=f32)
            scale = gain[:, here]
            scaled[:, here] = d * scale
            both = d * tok[:, here].astype(f32)
            with_gain = both * scale
            total = with_gain[:, :128]
            for k in range(1, width // 128):
                total = total + with_gain[:, k * 128 : (k + 1) * 128]
            projected[...] += total
            inv = inverse[...]
            for k in range(width // 128):
                cols = pl.ds(pl.multiple_of(i * width + k * 128, 128), 128)
                gain_own[dy, :, cols] = jnp.sum(
                    both[:, k * 128 : (k + 1) * 128] * inv, axis=0, keepdims=True
                )

    def finish():
        step = 64

        @pl.loop(0, rows // step)
        def _(i):
            here = pl.ds(pl.multiple_of(i * step, step), step)
            inv = inverse[here, 0:1]
            mean = jnp.sum(projected[here, :], axis=1, keepdims=True) / features
            back = inv * inv * inv * mean

            for j in range(features // 1024):
                cols = pl.ds(j * 1024, 1024)
                wide = tok[here, cols].astype(f32)
                tok[here, cols] = (inv * scaled[here, cols] - wide * back).astype(bf16)

    def gain_chip_sum(dy):
        total = gain_own[dy] + gain_core[dy]
        if dy:
            gain_chip[dy] = total
        else:
            gain_y[0] = total

    def gain_y_sum():
        gain_z[0] = gain_y[0] + gain_y[1] + gain_y[2] + gain_y[3]

    def gain_z_sum():
        total = gain_z[0] + gain_z[1] + gain_z[2] + gain_z[3]
        which = 2 * z + core
        chosen_part = total[:, :block]
        for i in range(1, 2 * RING):
            chosen_part = jnp.where(
                which == i, total[:, i * block : (i + 1) * block], chosen_part
            )
        gain_out[...] = chosen_part

    piece = difference.shape[1] // RING

    def quarter(i):
        return difference.at[:, pl.ds(pl.multiple_of(i * piece, 128), piece)]

    env.quarter = quarter

    def differ():
        for c in fragment_copies:
            c.wait()
        index = chosen[0]
        difference[...] = anchor_in[pl.ds(index, 1), :] - replica_in[pl.ds(index, 1), :]
        x_in[x] = quarter(x)[...]

    def add_x():
        z_out[...] = x_in[0] + x_in[1] + x_in[2] + x_in[3]

    def add_z():
        total[x] = z_out[...] + z_in[...]

    def update():
        index = chosen[0]
        for i in range(RING):
            here = pl.ds(i * piece, piece)
            pseudo = total[i] / 8
            momentum = MOMENTUM * velocity_in[pl.ds(index, 1), here] + pseudo
            momentum_out[:, here] = momentum
            param_out[:, here] = anchor_in[pl.ds(index, 1), here] - OUTER_RATE * (
                pseudo + MOMENTUM * momentum
            )

    for fn in (
        start_rest,
        square,
        turn,
        multiply,
        project,
        finish,
        gain_chip_sum,
        gain_y_sum,
        gain_z_sum,
        differ,
        add_x,
        add_z,
        update,
    ):
        setattr(env, fn.__name__, fn)

    order = plan(env)
    numbers = {}
    for e in order:
        for key, _, _, _ in e.sends:
            numbers[key] = len(numbers)

    def copy(key, src, dst, target):
        return pltpu.make_async_remote_copy(
            src_ref=src,
            dst_ref=dst,
            send_sem=send_sem.at[numbers[key]],
            recv_sem=recv_sem.at[numbers[key]],
            device_id=target,
            device_id_type=MESH,
        )

    sent, arrived = {}, []
    for number, e in enumerate(order):
        while arrived and arrived[0][0] < number - LAG:
            sent.pop(arrived.pop(0)[1]).wait_send()
        for key, refs in e.needs:
            dst, target = refs()
            copy(key, dst, dst, target).wait_recv()
            arrived.append((number, key))
        e.body()
        for key, _, _, refs in e.sends:
            sent[key] = copy(key, *refs())
            sent[key].start()
    for c in sent.values():
        c.wait_send()


def write_out(*refs):
    count = len(refs) // 2
    sem = refs[-1]
    step = refs[0].shape[0] // PIECES
    copies = [
        pltpu.make_async_copy(
            refs[0].at[pl.ds(i * step, step)],
            refs[count].at[pl.ds(i * step, step)],
            sem.at[count + i],
        )
        for i in range(PIECES)
    ]
    copies += [
        pltpu.make_async_copy(refs[i], refs[count + i], sem.at[i])
        for i in range(1, count)
    ]
    for c in copies:
        c.start()
    for c in copies:
        c.wait()


def local(
    tokens,
    norm_gain,
    value_weight,
    value_cotangent,
    local_fragments,
    global_fragments,
    outer_velocity,
    fragment_index,
):
    _, rows, features = tokens.shape
    _, block, values = value_weight.shape
    blocks = RING * RING
    fragments, length = global_fragments.shape
    span = features // RING
    vmem = pltpu.VMEM
    bf16, f32 = jnp.bfloat16, jnp.float32

    def plan(env):
        events = build(env, rows, features, block)
        return [events[i] for i in ORDER]

    sems = sum(len(e.sends) for e in plan(None))
    scratch = [
        vmem((1, features), f32),
        vmem((blocks, 2, block, rows), bf16),
        vmem((blocks, block, rows), bf16),
        vmem((2, rows, values), bf16),
        vmem((features, values), bf16),
        vmem((blocks, block, values), f32),
        vmem((rows, features), f32),
        vmem((rows, 128), f32),
        vmem((rows, 128), f32),
        vmem((RING, 1, span), f32),
        vmem((RING, 1, span), f32),
        vmem((RING, 1, span), f32),
        vmem((RING, 1, span), f32),
        vmem((RING, 1, span), f32),
        vmem((fragments, length), f32),
        vmem((fragments, length), f32),
        vmem((fragments, length), f32),
        vmem((1, length), f32),
        vmem((RING, 1, length // RING), f32),
        vmem((1, length // RING), f32),
        vmem((1, length // RING), f32),
        vmem((RING, 1, length // RING), f32),
    ]
    for lo, hi, _ in SCATTER_PARTS:
        size = hi - lo
        scratch += [
            vmem((RING, size, values), bf16),
            vmem((RING, size, values), bf16),
            vmem((2, RING, size, values), bf16),
            vmem((2, RING, size, values), bf16),
            vmem((size, values), bf16),
            vmem((size, values), bf16),
            vmem((2, size, values), bf16),
            vmem((2, size, values), bf16),
            vmem((RING, size, values), f32),
        ]
    scratch += [
        pltpu.SemaphoreType.DMA((sems,)),
        pltpu.SemaphoreType.DMA((sems,)),
        pltpu.SemaphoreType.DMA((8,)),
    ]
    in_vmem = pl.BlockSpec(memory_space=pltpu.VMEM)
    in_hbm = pl.BlockSpec(memory_space=pltpu.HBM)
    shapes = [
        ((rows, features), bf16),
        ((block, values), f32),
        ((1, block), f32),
        ((1, length), f32),
        ((1, length), f32),
    ]
    keep = functools.partial(pltpu.with_memory_space_constraint, memory_space=pltpu.HBM)
    results = pl.pallas_call(
        functools.partial(kernel, plan),
        out_shape=[vmem(*s) for s in shapes],
        in_specs=[in_hbm] * 7 + [pl.BlockSpec(memory_space=pltpu.SMEM)],
        out_specs=[in_vmem] * len(shapes),
        scratch_shapes=scratch,
        compiler_params=pltpu.CompilerParams(
            collective_id=0, has_side_effects=True, vmem_limit_bytes=42 * 2**20
        ),
        cost_estimate=pl.CostEstimate(
            flops=4 * rows * features * values, bytes_accessed=2**24, transcendentals=0
        ),
    )(
        keep(tokens[0]),
        keep(norm_gain),
        keep(value_weight[0]),
        keep(value_cotangent[0]),
        keep(local_fragments[0]),
        keep(global_fragments),
        keep(outer_velocity),
        fragment_index,
    )
    results = [pltpu.with_memory_space_constraint(r, pltpu.VMEM) for r in results]
    token_grad, weight_grad, gain_grad, param, momentum = pl.pallas_call(
        write_out,
        out_shape=[jax.ShapeDtypeStruct(*s) for s in shapes],
        in_specs=[in_vmem] * len(shapes),
        out_specs=[in_hbm] * len(shapes),
        scratch_shapes=[pltpu.SemaphoreType.DMA((len(shapes) + PIECES,))],
        compiler_params=pltpu.CompilerParams(vmem_limit_bytes=2**20),
    )(*results)
    return (
        token_grad[None],
        weight_grad[None],
        gain_grad,
        param.reshape(-1),
        momentum.reshape(-1),
    )


def solution(mesh):
    placed = (
        P("worker", "fsdp", None),
        P("worker", None),
        P("worker", "fsdp", None),
        P("worker", "fsdp", None),
        P("worker", None, "fsdp"),
        P(None, "fsdp"),
        P(None, "fsdp"),
        P(),
    )
    return jax.shard_map(
        local,
        mesh=mesh,
        in_specs=placed,
        out_specs=(
            P("worker", "fsdp", None),
            P("worker", "fsdp", None),
            P("worker", "fsdp"),
            P("fsdp"),
            P("fsdp"),
        ),
        check_vma=False,
    )
```

```python
import functools
import types

import jax
import jax.numpy as jnp
from jax import lax
from jax.experimental import pallas as pl
from jax.experimental.pallas import tpu as pltpu
from jax.sharding import PartitionSpec as P

EPSILON = 1e-05
MOMENTUM = 0.9
OUTER_RATE = 0.7
MESH = pl.DeviceIdType.MESH
RING = 4
NT = (((1,), (1,)), ((), ()))
GATHER_PARTS = ((0, 224, "z"),)
SCATTER_PARTS = ((0, 128, "y"), (128, 224, "z"))
WIDTH = 512
LAG = 12
PIECES = 4
ORDER = (
    0, 16, 17, 18, 20, 22, 24, 19, 34, 21, 58, 78, 23, 25, 42, 74, 38, 54, 4, 5, 26, 27, 36, 35,
    75, 1, 2, 28, 66, 29, 62, 55, 3, 60, 37, 30, 32, 59, 8, 7, 56, 50, 31, 76, 63, 64, 33, 10,
    11, 79, 14, 13, 39, 40, 6, 67, 43, 81, 44, 9, 83, 12, 46, 68, 57, 70, 15, 82, 85, 41, 84,
    51, 86, 45, 52, 47, 48, 77, 65, 61, 71, 80, 72, 87, 89, 49, 69, 73, 53, 88,
)
OPPOSITE = {1: 3, 3: 1, 2: 2}
CHUNKS = ((2, 1), (1, 1), (3, 1), (2, 0), (0, 1), (1, 0), (3, 0), (0, 0))


class Event:
    def __init__(self, name, body, cost, rank, needs=(), after=(), sends=()):
        self.name, self.body, self.cost, self.rank = name, body, cost, rank
        self.needs, self.after, self.sends = list(needs), list(after), list(sends)


def build(env, rows, features, block):
    events = []

    def add(name, *args, **kw):
        events.append(Event(name, *args, **kw))

    def nothing():
        pass

    chunk_of = {c: i for i, c in enumerate(CHUNKS)}

    def product(dy, dz):
        sides = {0: (0,), 2: (1,), 1: (0, 1), 3: (0, 1)}[dz]
        return [("product", chunk_of[dy, s]) for s in sides]

    def gather(number, lo, hi, first):
        mid = lo + (hi - lo) // 32 * 16
        halves = {1: (lo, mid), 3: (mid, hi)}
        second = "y" if first == "z" else "z"
        full_size = (hi - lo) * WIDTH * 2
        half_size = {1: (mid - lo) * WIDTH * 2, 3: (hi - mid) * WIDTH * 2}

        def offset(a, b):
            return (b, a) if first == "z" else (a, b)

        def target(axis, s):
            return env.device(0, s) if axis == "z" else env.device(s, 0)

        def held(a, b, span=(lo, hi), other=False):
            which = 1 - env.core if other else env.core
            return env.slot(*offset(a, b), which, *span)

        def whole(key, axis, s, a, b, own=False):
            def refs():
                here = held(a, b)
                src = env.weight.at[pl.ds(lo, hi - lo)] if own else here
                return src, here, target(axis, s)

            return (number, *key), axis + str(s), full_size, refs

        def half(key, axis, s, a, b):
            def refs():
                here = held(a, b, halves[s])
                return here, here, target(axis, s)

            return (number, *key), axis + str(s), half_size[s], refs

        def exchange(a, b, own=False):
            def refs():
                here = held(a, b)
                src = env.weight.at[pl.ds(lo, hi - lo)] if own else here
                return src, here, env.partner

            return (number, "x", a, b), "c", full_size, refs

        def need(key, axis, s, a, b, part=False):
            def refs():
                return held(a, b, halves[s] if part else (lo, hi)), target(axis, s)

            return (number, *key), refs

        def spread(a, own=False):
            return [whole(("b", a, s), second, s, a, 0, own) for s in (1, 3)]

        add(
            (number, "begin"),
            nothing,
            0.1,
            0,
            sends=[whole(("a", s), first, s, 0, 0, True) for s in (1, 3)]
            + spread(0, True)
            + [exchange(0, 0, True)],
        )
        for s in (1, 3):
            a = OPPOSITE[s]
            add(
                (number, "first", s),
                nothing,
                0.1,
                1,
                needs=[need(("a", s), first, s, a, 0)],
                sends=[half(("af", s), first, s, a, 0), *spread(a), exchange(a, 0)],
            )
        add(
            (number, "first", 2),
            nothing,
            0.1,
            1,
            needs=[need(("af", s), first, s, 2, 0, True) for s in (1, 3)],
            sends=[*spread(2), exchange(2, 0)],
        )
        for a in (0, 3, 1, 2):
            for s in (1, 3):
                b = OPPOSITE[s]
                add(
                    (number, "second", a, s),
                    nothing,
                    0.1,
                    1,
                    needs=[need(("b", a, s), second, s, a, b)],
                    sends=[half(("bf", a, s), second, s, a, b), exchange(a, b)],
                )
            add(
                (number, "second", a, 2),
                nothing,
                0.1,
                1,
                needs=[need(("bf", a, s), second, s, a, 2, True) for s in (1, 3)],
                sends=[exchange(a, 2)],
            )

        def settled(dy):
            needs = []
            for dz in range(RING):
                a, b = (dz, dy) if first == "z" else (dy, dz)

                def refs(a=a, b=b):
                    return held(a, b, other=True), env.partner

                needs.append(((number, "x", a, b), refs))
            return needs

        return settled

    settled = [gather(("g", i), *part) for i, part in enumerate(GATHER_PARTS)]

    chunk_bytes = 2 * block * rows * 2

    def turn_refs(i):
        def refs():
            span = pl.ds(2 * env.chunk(*CHUNKS[i]), 2)
            return (
                env.turned.at[span, 1 - env.core],
                env.turned_other.at[span],
                env.partner,
            )

        return refs

    def turn_need(i):
        def refs():
            return turn_refs(i)()[1], env.partner

        return ("t", i), refs

    add(
        "cot",
        lambda: env.start_rest(),
        0.4,
        0,
        sends=[
            (
                "cot",
                "c",
                rows * WIDTH * 2,
                lambda: (env.cotangent, env.cot.at[1], env.partner),
            )
        ],
    )
    add("square", lambda: env.square(), 2.5, 2, after=["cot"])
    for i in range(len(CHUNKS)):
        add(
            ("turn", i),
            lambda i=i: env.turn(env.chunk(*CHUNKS[i])),
            0.4,
            0.5,
            after=["square"] + ([("turn", i - 1)] if i else []),
            sends=[(("t", i), "c", chunk_bytes, turn_refs(i))],
        )
        needs = [turn_need(i)]
        if i == 0:
            needs.append(("cot", lambda: (env.cot.at[1], env.partner)))
        add(
            ("product", i),
            lambda i=i: env.multiply(env.chunk(*CHUNKS[i])),
            0.15,
            2.5,
            needs=needs,
            after=[("product", i - 1)] if i else [],
        )

    def scatter(number, lo, hi, first):
        size = hi - lo
        second = "y" if first == "z" else "z"
        mid = size // 32 * 16
        halves = {1: pl.ds(0, mid), 3: pl.ds(mid, size - mid)}
        index = {1: 0, 3: 1}
        spans = {1: pl.ds(lo, mid), 3: pl.ds(lo + mid, size - mid)}
        whole_size = size * WIDTH * 2
        half_size = {1: mid * WIDTH * 2, 3: (size - mid) * WIDTH * 2}
        bf16, f32 = jnp.bfloat16, jnp.float32

        def offset(a, b):
            return (b, a) if first == "z" else (a, b)

        def target(axis, s):
            return env.device(0, s) if axis == "z" else env.device(s, 0)

        def mine(a, b, s=None):
            span = pl.ds(lo, size) if s is None else spans[s]
            return env.part[env.chip[offset(a, b)], span, :]

        def bufs():
            return env.scatter[number[1]]

        def far_refs(b, s):
            r = bufs()
            return (
                r.far_out.at[b, halves[s]],
                r.far_in.at[b, halves[s]],
                target(first, s),
            )

        def near_refs(b, s):
            r = bufs()
            return r.near_out.at[index[s], b], r.near_in.at[index[s], b], target(first, s)

        def far2_refs(s):
            r = bufs()
            return r.far2_out.at[halves[s]], r.far2_in.at[halves[s]], target(second, s)

        def near2_refs(s):
            r = bufs()
            return r.near2_out.at[index[s]], r.near2_in.at[index[s]], target(second, s)

        def need(key, fn, *args):
            return (number, *key), lambda: fn(*args)[1:]

        def far(b):
            for s in (1, 3):
                bufs().far_out[b, halves[s], :] = mine(2, b, s).astype(bf16)

        def near(b, s):
            r, i = bufs(), index[s]
            r.near_out[i, b, halves[OPPOSITE[s]], :] = mine(s, b, OPPOSITE[s]).astype(bf16)
            r.near_out[i, b, halves[s], :] = (
                mine(s, b, s) + r.far_in[b, halves[s], :].astype(f32)
            ).astype(bf16)

        def gathered(b):
            r = bufs()
            r.total[b] = (
                mine(0, b) + r.near_in[0, b].astype(f32) + r.near_in[1, b].astype(f32)
            )

        def far2():
            r = bufs()
            for s in (1, 3):
                r.far2_out[halves[s], :] = r.total[2, halves[s], :].astype(bf16)

        def near2(s):
            r, i, o = bufs(), index[s], halves[OPPOSITE[s]]
            r.near2_out[i, o, :] = r.total[s, o, :].astype(bf16)
            r.near2_out[i, halves[s], :] = (
                r.total[s, halves[s], :] + r.far2_in[halves[s], :].astype(f32)
            ).astype(bf16)

        def final():
            r = bufs()
            env.weight_out[pl.ds(lo, size), :] = (
                r.total[0] + r.near2_in[0].astype(f32) + r.near2_in[1].astype(f32)
            )

        for b in (2, 1, 3, 0):
            add(
                (number, "far", b),
                functools.partial(far, b),
                0.15,
                2,
                after=product(*offset(2, b)),
                sends=[
                    (
                        (number, "f", b, s),
                        first + str(s),
                        half_size[s],
                        functools.partial(far_refs, b, s),
                    )
                    for s in (1, 3)
                ],
            )
            for s in (1, 3):
                add(
                    (number, "near", b, s),
                    functools.partial(near, b, s),
                    0.12,
                    2,
                    needs=[need(("f", b, s), far_refs, b, s)],
                    after=product(*offset(s, b)) + [(number, "far", b)],
                    sends=[
                        (
                            (number, "n", b, s),
                            first + str(s),
                            whole_size,
                            functools.partial(near_refs, b, s),
                        )
                    ],
                )
            add(
                (number, "sum", b),
                functools.partial(gathered, b),
                0.2,
                2,
                needs=[need(("n", b, s), near_refs, b, s) for s in (1, 3)],
                after=product(*offset(0, b)),
            )
        add(
            (number, "far2"),
            far2,
            0.1,
            2,
            after=[(number, "sum", 2)],
            sends=[
                (
                    (number, "f2", s),
                    second + str(s),
                    half_size[s],
                    functools.partial(far2_refs, s),
                )
                for s in (1, 3)
            ],
        )
        for s in (1, 3):
            add(
                (number, "near2", s),
                functools.partial(near2, s),
                0.2,
                2,
                needs=[need(("f2", s), far2_refs, s)],
                after=[(number, "sum", s)],
                sends=[
                    (
                        (number, "n2", s),
                        second + str(s),
                        whole_size,
                        functools.partial(near2_refs, s),
                    )
                ],
            )
        add(
            (number, "final"),
            final,
            0.3,
            2,
            needs=[need(("n2", s), near2_refs, s) for s in (1, 3)],
            after=[(number, "sum", 0)],
        )

    for i, part in enumerate(SCATTER_PARTS):
        scatter(("s", i), *part)

    def x_from(d):
        return lax.rem(env.x + RING - d, RING)

    def x_refs(d):
        return env.quarter(lax.rem(env.x + d, RING)), env.x_in.at[env.x], env.beside_x(d)

    def x_need(d):
        return ("ox", d), lambda: (env.x_in.at[x_from(d)], env.beside_x(d))

    def all_refs(d):
        return env.total.at[env.x], env.total.at[env.x], env.beside_x(d)

    def all_need(d):
        return ("oa", d), lambda: (env.total.at[x_from(d)], env.beside_x(d))

    def to_x(key, refs):
        return [
            ((key, d), "x" + str(d), 16384, functools.partial(refs, d)) for d in (1, 2, 3)
        ]

    add(
        "outer",
        lambda: env.differ(),
        0.5,
        2.2,
        after=["square"],
        sends=to_x("ox", x_refs),
    )
    add(
        "outer2",
        lambda: env.add_x(),
        0.2,
        4,
        needs=[x_need(d) for d in (1, 2, 3)],
        sends=[("oz", "z1", 8192, lambda: (env.z_out, env.z_in, env.beside_low))],
    )
    add(
        "outer3",
        lambda: env.add_z(),
        0.1,
        4,
        needs=[("oz", lambda: (env.z_in, env.beside_low))],
        sends=to_x("oa", all_refs),
    )
    add(
        "outer4",
        lambda: env.update(),
        0.6,
        4,
        needs=[all_need(d) for d in (1, 2, 3)],
    )

    add("own", lambda: env.own_copy.wait(), 0.0, 2, after=["square"])
    gain_bytes = features // RING * 4
    for dy in (0, 1, 3, 2):
        add(
            ("project", dy),
            functools.partial(lambda dy: env.project(dy), dy),
            1.0,
            2.8,
            needs=[n for fn in settled for n in fn(dy)],
            after=["own"],
            sends=[
                (
                    ("gc", dy),
                    "c",
                    gain_bytes,
                    lambda dy=dy: (env.gain_own.at[dy], env.gain_core.at[dy], env.partner),
                )
            ],
        )
        if dy:
            sends = [
                (
                    ("gy", dy),
                    "y" + str(dy) if dy != 2 else "y1",
                    gain_bytes,
                    lambda dy=dy: (
                        env.gain_chip.at[dy],
                        env.gain_y.at[dy],
                        env.device(dy, 0),
                    ),
                )
            ]
        else:
            sends = []
        add(
            ("gain", dy),
            functools.partial(lambda dy: env.gain_chip_sum(dy), dy),
            0.1,
            1,
            needs=[
                (("gc", dy), lambda dy=dy: (env.gain_core.at[dy], env.partner))
            ],
            after=[("project", dy)],
            sends=sends,
        )
    add(
        "gain y",
        lambda: env.gain_y_sum(),
        0.1,
        1,
        needs=[
            (("gy", d), lambda d=d: (env.gain_y.at[d], env.device(d, 0))) for d in (1, 2, 3)
        ],
        after=[("gain", 0)],
        sends=[
            (
                ("gz", d),
                "z" + str(d) if d != 2 else "z1",
                gain_bytes,
                lambda d=d: (env.gain_z.at[0], env.gain_z.at[d], env.device(0, d)),
            )
            for d in (1, 2, 3)
        ],
    )
    add(
        "gain z",
        lambda: env.gain_z_sum(),
        0.2,
        3,
        needs=[
            (("gz", d), lambda d=d: (env.gain_z.at[d], env.device(0, d))) for d in (1, 2, 3)
        ],
    )
    add(
        "finish",
        lambda: env.finish(),
        2.0,
        2.9,
        after=[("project", dy) for dy in range(RING)],
    )
    return events


def kernel(
    plan,
    tokens,
    gain_all,
    weight,
    cotangent,
    replica_part,
    anchor,
    velocity,
    chosen,
    token_out,
    weight_out,
    gain_out,
    param_out,
    momentum_out,
    gain,
    turned,
    turned_other,
    cot,
    full,
    part,
    scaled,
    inverse,
    projected,
    gain_own,
    gain_core,
    gain_chip,
    gain_y,
    gain_z,
    replica_in,
    anchor_in,
    velocity_in,
    difference,
    x_in,
    z_out,
    z_in,
    total,
    *rest,
):
    buffers, (send_sem, recv_sem, local_sem) = rest[:-3], rest[-3:]
    rows, features = token_out.shape
    block = weight.shape[0]
    f32, bf16 = jnp.float32, jnp.bfloat16
    tok = token_out

    worker = lax.axis_index("worker")
    place = lax.axis_index("fsdp")
    core = lax.rem(place, 2)
    z = lax.rem(place // 2, RING)
    y = place // (2 * RING)
    x, low = worker // 2, lax.rem(worker, 2)

    env = types.SimpleNamespace(
        core=core,
        x=x,
        weight=weight,
        cotangent=cotangent,
        cot=cot,
        turned=turned,
        turned_other=turned_other,
        part=part,
        x_in=x_in,
        z_out=z_out,
        z_in=z_in,
        total=total,
        weight_out=weight_out,
        gain_own=gain_own,
        gain_core=gain_core,
        gain_chip=gain_chip,
        gain_y=gain_y,
        gain_z=gain_z,
    )
    env.chip = {
        (dy, dz): lax.rem(y + dy, RING) * RING + lax.rem(z + dz, RING)
        for dy in range(RING)
        for dz in range(RING)
    }
    env.device = lambda dy, dz: {"fsdp": 2 * env.chip[dy, dz] + core}
    env.partner = {"fsdp": place + 1 - 2 * core}
    env.beside_x = lambda d: {"worker": lax.rem(x + d, RING) * 2 + low}
    env.beside_low = {"worker": x * 2 + 1 - low}
    env.chunk = lambda dy, far: lax.rem(y + dy, RING) * 2 + (
        1 - z // 2 if far else z // 2
    )
    names = ["far_out", "far_in", "near_out", "near_in"]
    names += ["far2_out", "far2_in", "near2_out", "near2_in", "total"]
    env.scatter = [
        types.SimpleNamespace(**dict(zip(names, buffers[9 * i : 9 * i + 9])))
        for i in range(len(SCATTER_PARTS))
    ]

    def slot(dy, dz, which, lo, hi):
        start = (2 * env.chip[dy, dz] + which) * block + lo
        return full.at[pl.ds(pl.multiple_of(start, 16), hi - lo)]

    env.slot = slot

    half_rows = rows // 2
    token_copies = []
    for i in range(2):
        span = pl.ds(i * half_rows, half_rows)
        token_copies.append(
            pltpu.make_async_copy(tokens.at[span], tok.at[span], local_sem.at[i])
        )
    cot_copy = pltpu.make_async_copy(cotangent, cot.at[0], local_sem.at[2])
    gain_copy = pltpu.make_async_copy(gain_all, gain, local_sem.at[7])
    own = pl.ds(pl.multiple_of(place * block, 16), block)
    env.own_copy = pltpu.make_async_copy(weight, full.at[own], local_sem.at[3])
    fragment_copies = [
        pltpu.make_async_copy(src, dst, local_sem.at[4 + i])
        for i, (src, dst) in enumerate(
            ((replica_part, replica_in), (anchor, anchor_in), (velocity, velocity_in))
        )
    ]
    greeted = [env.device(0, d) for d in (1, 3, 2)]
    greeted += [env.device(d, 0) for d in (1, 3, 2)]
    greeted += [env.partner, env.beside_low]
    greeted += [env.beside_x(d) for d in (1, 2, 3)]
    barrier = pltpu.get_barrier_semaphore()
    for target in greeted:
        pl.semaphore_signal(barrier, inc=1, device_id=target, device_id_type=MESH)
    for c in token_copies:
        c.start()
    pl.semaphore_wait(barrier, len(greeted))

    def start_rest():
        for c in (gain_copy, cot_copy, env.own_copy, *fragment_copies):
            c.start()

    def square():
        projected[...] = jnp.zeros_like(projected)
        for c in (gain_copy, cot_copy):
            c.wait()
        for i in range(2):
            token_copies[i].wait()
            here = pl.ds(i * half_rows, half_rows)

            def step(j, total):
                wide = tok[here, pl.ds(pl.multiple_of(j * 256, 128), 256)].astype(f32)
                wide = wide * wide
                return total + wide[:, :128] + wide[:, 128:]

            total = lax.fori_loop(
                0, features // 256, step, jnp.zeros((half_rows, 128), f32)
            )
            inv = lax.rsqrt(jnp.sum(total, axis=1, keepdims=True) / features + EPSILON)
            inverse[here, :] = jnp.broadcast_to(inv, (half_rows, 128))

    def turn(j):
        width = 4 * block
        cols = pl.ds(pl.multiple_of(j * width, 128), width)
        for i in range(2):
            here = pl.ds(i * half_rows, half_rows)
            inv = inverse[here, 0:1]
            normed = (tok[here, cols].astype(f32) * inv * gain[:, cols]).astype(bf16)
            flipped = normed.T
            for b in range(4):
                turned[2 * j + b // 2, b % 2, :, here] = flipped[
                    b * block : (b + 1) * block
                ]
        for k in range(2):
            part[2 * j + k] = jnp.dot(
                turned[2 * j + k, core], cot[0], preferred_element_type=f32
            )

    def multiply(j):
        for k in range(2):
            part[2 * j + k] += jnp.dot(
                turned_other[2 * j + k], cot[1], preferred_element_type=f32
            )

    span = features // RING
    width = span // 2

    def project(dy):
        start = pl.multiple_of(lax.rem(y + dy, RING) * span, 128)

        @pl.loop(0, 2)
        def _(i):
            here = pl.ds(pl.multiple_of(start + i * width, 128), width)
            d = lax.dot_general(cot[0], full[here, :], NT, preferred_element_type=f32)
            scale = gain[:, here]
            scaled[:, here] = d * scale
            both = d * tok[:, here].astype(f32)
            with_gain = both * scale
            total = with_gain[:, :128]
            for k in range(1, width // 128):
                total = total + with_gain[:, k * 128 : (k + 1) * 128]
            projected[...] += total
            inv = inverse[...]
            for k in range(width // 128):
                cols = pl.ds(pl.multiple_of(i * width + k * 128, 128), 128)
                gain_own[dy, :, cols] = jnp.sum(
                    both[:, k * 128 : (k + 1) * 128] * inv, axis=0, keepdims=True
                )

    def finish():
        step = 64

        @pl.loop(0, rows // step)
        def _(i):
            here = pl.ds(pl.multiple_of(i * step, step), step)
            inv = inverse[here, 0:1]
            mean = jnp.sum(projected[here, :], axis=1, keepdims=True) / features
            back = inv * inv * inv * mean

            for j in range(features // 1024):
                cols = pl.ds(j * 1024, 1024)
                wide = tok[here, cols].astype(f32)
                tok[here, cols] = (inv * scaled[here, cols] - wide * back).astype(bf16)

    def gain_chip_sum(dy):
        total = gain_own[dy] + gain_core[dy]
        if dy:
            gain_chip[dy] = total
        else:
            gain_y[0] = total

    def gain_y_sum():
        gain_z[0] = gain_y[0] + gain_y[1] + gain_y[2] + gain_y[3]

    def gain_z_sum():
        total = gain_z[0] + gain_z[1] + gain_z[2] + gain_z[3]
        which = 2 * z + core
        chosen_part = total[:, :block]
        for i in range(1, 2 * RING):
            chosen_part = jnp.where(
                which == i, total[:, i * block : (i + 1) * block], chosen_part
            )
        gain_out[...] = chosen_part

    piece = difference.shape[1] // RING

    def quarter(i):
        return difference.at[:, pl.ds(pl.multiple_of(i * piece, 128), piece)]

    env.quarter = quarter

    def differ():
        for c in fragment_copies:
            c.wait()
        index = chosen[0]
        difference[...] = anchor_in[pl.ds(index, 1), :] - replica_in[pl.ds(index, 1), :]
        x_in[x] = quarter(x)[...]

    def add_x():
        z_out[...] = x_in[0] + x_in[1] + x_in[2] + x_in[3]

    def add_z():
        total[x] = z_out[...] + z_in[...]

    def update():
        index = chosen[0]
        for i in range(RING):
            here = pl.ds(i * piece, piece)
            pseudo = total[i] / 8
            momentum = MOMENTUM * velocity_in[pl.ds(index, 1), here] + pseudo
            momentum_out[:, here] = momentum
            param_out[:, here] = anchor_in[pl.ds(index, 1), here] - OUTER_RATE * (
                pseudo + MOMENTUM * momentum
            )

    for fn in (
        start_rest,
        square,
        turn,
        multiply,
        project,
        finish,
        gain_chip_sum,
        gain_y_sum,
        gain_z_sum,
        differ,
        add_x,
        add_z,
        update,
    ):
        setattr(env, fn.__name__, fn)

    order = plan(env)
    numbers = {}
    for e in order:
        for key, _, _, _ in e.sends:
            numbers[key] = len(numbers)

    def copy(key, src, dst, target):
        return pltpu.make_async_remote_copy(
            src_ref=src,
            dst_ref=dst,
            send_sem=send_sem.at[numbers[key]],
            recv_sem=recv_sem.at[numbers[key]],
            device_id=target,
            device_id_type=MESH,
        )

    sent, arrived = {}, []
    for number, e in enumerate(order):
        while arrived and arrived[0][0] < number - LAG:
            sent.pop(arrived.pop(0)[1]).wait_send()
        for key, refs in e.needs:
            dst, target = refs()
            copy(key, dst, dst, target).wait_recv()
            arrived.append((number, key))
        e.body()
        for key, _, _, refs in e.sends:
            sent[key] = copy(key, *refs())
            sent[key].start()
    for c in sent.values():
        c.wait_send()


def write_out(*refs):
    count = len(refs) // 2
    sem = refs[-1]
    step = refs[0].shape[0] // PIECES
    copies = [
        pltpu.make_async_copy(
            refs[0].at[pl.ds(i * step, step)],
            refs[count].at[pl.ds(i * step, step)],
            sem.at[count + i],
        )
        for i in range(PIECES)
    ]
    copies += [
        pltpu.make_async_copy(refs[i], refs[count + i], sem.at[i])
        for i in range(1, count)
    ]
    for c in copies:
        c.start()
    for c in copies:
        c.wait()


def local(
    tokens,
    norm_gain,
    value_weight,
    value_cotangent,
    local_fragments,
    global_fragments,
    outer_velocity,
    fragment_index,
):
    _, rows, features = tokens.shape
    _, block, values = value_weight.shape
    blocks = RING * RING
    fragments, length = global_fragments.shape
    span = features // RING
    vmem = pltpu.VMEM
    bf16, f32 = jnp.bfloat16, jnp.float32

    def plan(env):
        events = build(env, rows, features, block)
        return [events[i] for i in ORDER]

    sems = sum(len(e.sends) for e in plan(None))
    scratch = [
        vmem((1, features), f32),
        vmem((blocks, 2, block, rows), bf16),
        vmem((blocks, block, rows), bf16),
        vmem((2, rows, values), bf16),
        vmem((features, values), bf16),
        vmem((blocks, block, values), f32),
        vmem((rows, features), f32),
        vmem((rows, 128), f32),
        vmem((rows, 128), f32),
        vmem((RING, 1, span), f32),
        vmem((RING, 1, span), f32),
        vmem((RING, 1, span), f32),
        vmem((RING, 1, span), f32),
        vmem((RING, 1, span), f32),
        vmem((fragments, length), f32),
        vmem((fragments, length), f32),
        vmem((fragments, length), f32),
        vmem((1, length), f32),
        vmem((RING, 1, length // RING), f32),
        vmem((1, length // RING), f32),
        vmem((1, length // RING), f32),
        vmem((RING, 1, length // RING), f32),
    ]
    for lo, hi, _ in SCATTER_PARTS:
        size = hi - lo
        scratch += [
            vmem((RING, size, values), bf16),
            vmem((RING, size, values), bf16),
            vmem((2, RING, size, values), bf16),
            vmem((2, RING, size, values), bf16),
            vmem((size, values), bf16),
            vmem((size, values), bf16),
            vmem((2, size, values), bf16),
            vmem((2, size, values), bf16),
            vmem((RING, size, values), f32),
        ]
    scratch += [
        pltpu.SemaphoreType.DMA((sems,)),
        pltpu.SemaphoreType.DMA((sems,)),
        pltpu.SemaphoreType.DMA((8,)),
    ]
    in_vmem = pl.BlockSpec(memory_space=pltpu.VMEM)
    in_hbm = pl.BlockSpec(memory_space=pltpu.HBM)
    shapes = [
        ((rows, features), bf16),
        ((block, values), f32),
        ((1, block), f32),
        ((1, length), f32),
        ((1, length), f32),
    ]
    keep = functools.partial(pltpu.with_memory_space_constraint, memory_space=pltpu.HBM)
    results = pl.pallas_call(
        functools.partial(kernel, plan),
        out_shape=[vmem(*s) for s in shapes],
        in_specs=[in_hbm] * 7 + [pl.BlockSpec(memory_space=pltpu.SMEM)],
        out_specs=[in_vmem] * len(shapes),
        scratch_shapes=scratch,
        compiler_params=pltpu.CompilerParams(
            collective_id=0, has_side_effects=True, vmem_limit_bytes=42 * 2**20
        ),
        cost_estimate=pl.CostEstimate(
            flops=4 * rows * features * values, bytes_accessed=2**24, transcendentals=0
        ),
    )(
        keep(tokens[0]),
        keep(norm_gain),
        keep(value_weight[0]),
        keep(value_cotangent[0]),
        keep(local_fragments[0]),
        keep(global_fragments),
        keep(outer_velocity),
        fragment_index,
    )
    results = [pltpu.with_memory_space_constraint(r, pltpu.VMEM) for r in results]
    token_grad, weight_grad, gain_grad, param, momentum = pl.pallas_call(
        write_out,
        out_shape=[jax.ShapeDtypeStruct(*s) for s in shapes],
        in_specs=[in_vmem] * len(shapes),
        out_specs=[in_hbm] * len(shapes),
        scratch_shapes=[pltpu.SemaphoreType.DMA((len(shapes) + PIECES,))],
        compiler_params=pltpu.CompilerParams(vmem_limit_bytes=2**20),
    )(*results)
    return (
        token_grad[None],
        weight_grad[None],
        gain_grad,
        param.reshape(-1),
        momentum.reshape(-1),
    )


def solution(mesh):
    placed = (
        P("worker", "fsdp", None),
        P("worker", None),
        P("worker", "fsdp", None),
        P("worker", "fsdp", None),
        P("worker", None, "fsdp"),
        P(None, "fsdp"),
        P(None, "fsdp"),
        P(),
    )
    return jax.shard_map(
        local,
        mesh=mesh,
        in_specs=placed,
        out_specs=(
            P("worker", "fsdp", None),
            P("worker", "fsdp", None),
            P("worker", "fsdp"),
            P("fsdp"),
            P("fsdp"),
        ),
        check_vma=False,
    )
```
